32 devices in a mesh: dp: 8 (over y, x, core), ctx: 4 (over z).
Axes of the slice: x: 2, y: 2, z: 4, core: 2. Of those that a mesh axis runs over, the one named last changes fastest.
Arguments:
- tokens: bfloat16 [8, 896, 2048], P('dp', 'ctx'), may hold values from -6 to 6
- norm_gain: bfloat16 [2048], replicated, may hold values from 0.099609375 to 1.8984375
- q_weight: bfloat16 [2048, 2048], P('dp'), may hold values from -0.110927376 to 0.110927376
- k_weight: bfloat16 [2048, 2048], P('dp'), may hold values from -6.408155204503087 to 6.408155204503087
- v_weight: bfloat16 [2048, 2048], P('dp'), may hold values from -0.125 to 0.125
Outputs:
- attended: bfloat16 [8, 896, 2048], P('dp', 'ctx')
The draws below stay inside these ranges and needn't reach their ends.
All inputs are finite; a program needn't handle non-finite values.
Results may differ from the reference program's by a relative error of at most 0.0055.
The reference program's roundings to bfloat16 on the way (of `normed`, `values` and `probs`) count: a program that leaves them out, or rounds other values in their place, can miss the bound.
Values may be sent and summed in bfloat16 or wider, within the bound.
No kernel may reach another device: no remote copies, remote signals or barrier semaphores. Data moves between devices by JAX's collectives and lax.ppermute only.
A program may use at most 128 MiB of HBM per device.

```python
import jax
import jax.numpy as jnp
from jax import lax

D = 2048
HEADS = 16
HEAD_DIM = 128
SEQS = 8
LEN = 896


def weight_pair(key):
    columns = HEADS * HEAD_DIM
    query = jnp.clip(jax.random.normal(jax.random.fold_in(key, 11), (D, columns), jnp.float32), -5.0, 5.0) * D ** (-0.5)
    other = jnp.clip(jax.random.normal(jax.random.fold_in(key, 12), (D, columns), jnp.float32), -5.0, 5.0) * D ** (-0.5)
    return (query, other)


def draw_q_weight(key, part):
    return weight_pair(key)[0].astype(jnp.bfloat16)


def draw_k_weight(key, part):
    return weight_pair(key)[1].astype(jnp.bfloat16)


def draw_tokens(key, part):
    base = jnp.clip(jax.random.normal(jax.random.fold_in(key, 21), (SEQS, LEN, D), jnp.float32), -6.0, 6.0)
    return base.astype(jnp.bfloat16)


def level_of(stream_key, shape, split, smallest, high):
    level = 1.0
    for position, parts in split:
        heights = jax.random.uniform(jax.random.fold_in(jax.random.fold_in(stream_key, 6), position), (parts,), jnp.float32, smallest / len(split), high / len(split))
        level = level * jnp.repeat(jnp.exp(heights), shape[position] // parts).reshape((-1,) + (1,) * (len(shape) - 1 - position))
    return level


def normal_values(key, shape, width, reach, shards=(), kind=jnp.bfloat16):
    result = width * jax.random.normal(key, shape, jnp.float32)
    if shards:
        result = result * level_of(key, shape, shards, -0.22, 0.18)
    return jnp.clip(result, -reach, reach).astype(kind)


def setup_inputs(seed: int = 0) -> dict:
    key_list = jax.random.split(jax.random.key(seed), 6)
    return {
        "tokens": draw_tokens(jax.random.fold_in(key_list[5], 71), 0),
        "norm_gain": jnp.clip(1.0 + 0.18 * jax.random.normal(key_list[1], (D,), jnp.float32), 0.099609375, 1.8984375).astype(jnp.bfloat16),
        "q_weight": draw_q_weight(jax.random.fold_in(key_list[5], 71), 0),
        "k_weight": draw_k_weight(jax.random.fold_in(key_list[5], 71), 0),
        "v_weight": normal_values(key_list[4], (D, HEADS * HEAD_DIM), D ** -0.5, 0.125, ((0, 8),)),
    }


def rotate(values, positions):
    half = HEAD_DIM // 2
    shaped = values.reshape(values.shape[0], HEADS, HEAD_DIM)
    freqs = 10000.0 ** (-(jnp.arange(half).astype(jnp.float32) * 2.0) / HEAD_DIM)
    angles = positions[:, None] * freqs[None, :]
    cosine = jnp.cos(angles)[:, None, :]
    sine = jnp.sin(angles)[:, None, :]
    first = shaped[:, :, :half]
    second = shaped[:, :, half:]
    turned = jnp.concatenate([first * cosine - second * sine, second * cosine + first * sine], axis=2)
    return turned.reshape(values.shape[0], HEADS * HEAD_DIM)

def one_sequence(sequence, norm_gain, q_weight, k_weight, v_weight):
    rows = sequence.astype(jnp.float32)
    scale_rows = lax.rsqrt(lax.optimization_barrier(jnp.mean(rows * rows, axis=1, keepdims=True)) + 1e-05)
    normed = (rows * scale_rows * norm_gain.astype(jnp.float32)[None, :]).astype(jnp.bfloat16)
    q_lin = jnp.dot(normed, q_weight, preferred_element_type=jnp.float32)
    k_lin = jnp.dot(normed, k_weight, preferred_element_type=jnp.float32)
    v_lin = jnp.dot(normed, v_weight, preferred_element_type=jnp.float32)
    values = v_lin.astype(jnp.bfloat16)
    positions = jnp.arange(LEN).astype(jnp.float32)
    queries = rotate(q_lin, positions).astype(jnp.bfloat16)
    keys = rotate(k_lin, positions).astype(jnp.bfloat16)
    head_q = queries.reshape(LEN, HEADS, HEAD_DIM).transpose(1, 0, 2)
    head_k = keys.reshape(LEN, HEADS, HEAD_DIM).transpose(1, 0, 2)
    head_v = values.reshape(LEN, HEADS, HEAD_DIM).transpose(1, 0, 2)
    allowed = jnp.arange(LEN)[None, :] <= jnp.arange(LEN)[:, None]
    factor = HEAD_DIM ** (-0.5)

    def one_head(triple):
        qa, ka, va = triple
        scores = jnp.dot(qa, ka.T, preferred_element_type=jnp.float32) * factor
        scores = jnp.where(allowed, scores, -1e+30)
        top = lax.optimization_barrier(jnp.max(scores, axis=1, keepdims=True))
        expo = jnp.where(allowed, jnp.exp(scores - top), 0.0)
        probs = expo.astype(jnp.bfloat16)
        numer = jnp.dot(probs, va, preferred_element_type=jnp.float32)
        return numer / lax.optimization_barrier(jnp.sum(expo, axis=1, keepdims=True))
    outputs = lax.map(one_head, (head_q, head_k, head_v))
    return outputs.transpose(1, 0, 2).reshape(LEN, HEADS * HEAD_DIM).astype(jnp.bfloat16)

def reference(tokens, norm_gain, q_weight, k_weight, v_weight):
    return lax.map(lambda sequence: one_sequence(sequence, norm_gain, q_weight, k_weight, v_weight), tokens)
```

```python
import functools
import math

import jax
import jax.numpy as jnp
from jax import lax
from jax.experimental import pallas as pl
from jax.experimental.pallas import tpu as pltpu
from jax.sharding import PartitionSpec as P

HEADS = 16
HEAD_DIM = 128
HALF = HEAD_DIM // 2
EPS = 1e-05
VMEM_LIMIT = 56 * 1024 * 1024


def tables(length):
    freqs = 10000.0 ** (-(jnp.arange(HALF).astype(jnp.float32) * 2.0) / HEAD_DIM)
    angles = jnp.arange(length).astype(jnp.float32)[:, None] * freqs[None, :]
    cosine = jnp.cos(angles)
    sine = jnp.sin(angles)
    return (
        jnp.concatenate([cosine, cosine], axis=1),
        jnp.concatenate([-sine, sine], axis=1),
    )


def normalize(block, gain):
    rows = block.astype(jnp.float32)
    scale = lax.rsqrt(jnp.mean(rows * rows, axis=1, keepdims=True) + EPS)
    return (rows * scale * gain.astype(jnp.float32)).astype(jnp.bfloat16)


def project(normed, weights, cos_ref, sin_ref, starts, rows, cols, store):
    step = 2 * HEAD_DIM
    for first in range(0, 3 * cols, step):
        linear = jnp.dot(
            normed[...], weights[:, first : first + step], preferred_element_type=jnp.float32
        )
        for block, start in enumerate(starts):
            part = linear[block * rows : (block + 1) * rows]
            if first < 2 * cols:
                cosine = cos_ref[pl.ds(start, rows), :]
                sine = sin_ref[pl.ds(start, rows), :]
                heads = [part[:, h * HEAD_DIM : (h + 1) * HEAD_DIM] for h in range(2)]
                part = jnp.concatenate(
                    [x * cosine + pltpu.roll(x, HALF, 1) * sine for x in heads], axis=1
                )
            store(block, first, step, part.astype(jnp.bfloat16))


def start_weights(owners, shards, weights, sems):
    depth = shards[0].shape[0]
    copies = []
    for i, (owner, shard) in enumerate(zip(owners, shards)):
        copy = pltpu.make_async_copy(
            shard, weights.at[pl.ds(pl.multiple_of(owner * depth, depth), depth)], sems.at[i]
        )
        copy.start()
        copies.append(copy)
    return copies


def early_kernel(spec, *refs):
    n, m, rows, cols = spec["blocks"], spec["shards"], spec["rows"], spec["cols"]
    tokens, shards = refs[:n], refs[n : n + m]
    gain, cos_ref, sin_ref, out, held, normed, weights, token_sems, weight_sems = refs[n + m :]
    place, owners = spec["places"](), spec["owners"]()
    loads = []
    for i in range(n):
        load = pltpu.make_async_copy(
            tokens[i], held.at[pl.ds(i * rows, rows)], token_sems.at[i]
        )
        load.start()
        loads.append(load)
    weight_loads = start_weights(owners, shards, weights, weight_sems)
    for i in range(n):
        loads[i].wait()
        part = pl.ds(i * rows, rows)
        normed[part, :] = normalize(held[part, :], gain[...])
    for load in weight_loads:
        load.wait()
    starts = [pl.multiple_of(place[i] * rows, rows) for i in range(n)]

    def store(block, first, step, value):
        out[pl.ds(block * rows, rows), pl.ds(first, step)] = value

    project(normed, weights, cos_ref, sin_ref, starts, rows, cols, store)


def late_kernel(spec, *refs):
    n, m, rows, cols = spec["blocks"], spec["shards"], spec["rows"], spec["cols"]
    total = spec["total"]
    tokens, shards = refs[:2], refs[2 : 2 + m]
    early, gain, cos_ref, sin_ref = refs[2 + m : 6 + m]
    outs = refs[6 + m : 6 + m + total]
    held, normed, weights, qkv, result, token_sems, weight_sems, early_sems, out_sems = refs[6 + m + total :]
    place, owners = spec["places"](), spec["owners"]()
    me = spec["me"]()
    inner = spec["inner"]()
    weight_loads = start_weights(owners, shards, weights, weight_sems)

    @pl.when(inner)
    def _():
        pltpu.make_async_copy(tokens[0], held, token_sems.at[0]).start()

    @pl.when(jnp.logical_not(inner))
    def _():
        pltpu.make_async_copy(tokens[1], held, token_sems.at[0]).start()

    early_loads = []
    for i in range(n):
        load = pltpu.make_async_copy(
            early.at[pl.ds(i * rows, rows)],
            qkv.at[pl.ds(pl.multiple_of(place[i] * rows, rows), rows)],
            early_sems.at[i],
        )
        load.start()
        early_loads.append(load)
    pltpu.make_async_copy(tokens[0], held, token_sems.at[0]).wait()
    normed[...] = normalize(held[...], gain[...])
    for load in weight_loads:
        load.wait()
    last = pl.multiple_of(place[n] * rows, rows)

    def store(block, first, step, value):
        qkv[pl.ds(last, rows), pl.ds(first, step)] = value

    project(normed, weights, cos_ref, sin_ref, [last], rows, cols, store)
    for load in early_loads:
        load.wait()
    attend(qkv, result, me, total, rows, cols)
    copies = []
    for k in range(total):
        copy = pltpu.make_async_copy(result.at[k], outs[k], out_sems.at[k])
        copy.start()
        copies.append(copy)
    for copy in copies:
        copy.wait()


def attend(qkv, result, me, total, rows, cols):
    factor = HEAD_DIM ** (-0.5) * math.log2(math.e)
    below = lax.broadcasted_iota(jnp.int32, (rows, rows), 0) >= lax.broadcasted_iota(
        jnp.int32, (rows, rows), 1
    )
    for head in range(cols // HEAD_DIM):
        for block in range(total):
            size = (block + 1) * rows
            q = qkv[block * rows : size, head * HEAD_DIM : (head + 1) * HEAD_DIM]
            k = qkv[0:size, cols + head * HEAD_DIM : cols + (head + 1) * HEAD_DIM]
            v = qkv[0:size, 2 * cols + head * HEAD_DIM : 2 * cols + (head + 1) * HEAD_DIM]
            scores = lax.dot_general(
                q, k, (((1,), (1,)), ((), ())), preferred_element_type=jnp.float32
            )
            own = jnp.where(below, scores[:, block * rows :], -1e30)
            scores = jnp.concatenate([scores[:, : block * rows], own], axis=1) if block else own
            top = jnp.max(scores, axis=1, keepdims=True)
            expo = jnp.exp2((scores - top) * factor)
            bottom = jnp.sum(expo, axis=1, keepdims=True)
            numer = jnp.dot(expo.astype(jnp.bfloat16), v, preferred_element_type=jnp.float32)
            result[block ^ me, :, head * HEAD_DIM : (head + 1) * HEAD_DIM] = (
                numer / bottom
            ).astype(jnp.bfloat16)


def join_kernel(spec, *refs):
    total, cols = spec["total"], spec["cols"]
    pieces, out, sems = refs[:total], refs[total], refs[total + 1]
    me = spec["me"]()
    copies = []
    for k in range(total):
        copy = pltpu.make_async_copy(
            pieces[k],
            out.at[0, :, pl.ds(pl.multiple_of((me ^ k) * cols, cols), cols)],
            sems.at[k],
        )
        copy.start()
        copies.append(copy)
    for copy in copies:
        copy.wait()


def block_plan(dp, ctx):
    flat = lambda d, c: d * ctx + c
    every = [(d, c) for d in range(dp) for c in range(ctx)]
    make = lambda to: [
        (flat(d, c), flat(*to(d, c))) for d, c in every if to(d, c) is not None
    ]
    return make


def fast(dp, ctx, tokens, norm_gain, q_weight, k_weight, v_weight):
    rows, features = tokens.shape[1], tokens.shape[2]
    depth = q_weight.shape[0]
    cols = HEADS // ctx * HEAD_DIM
    make = block_plan(dp, ctx)
    axes = ("dp", "ctx")
    send = lambda value, perm: lax.ppermute(value, axes, perm)
    me = lax.axis_index("ctx")
    own = tokens[0]
    part = jnp.concatenate(
        [lax.dynamic_slice_in_dim(w, me * cols, cols, 1) for w in (q_weight, k_weight, v_weight)], axis=1
    )
    pair = make(lambda d, c: (d, c ^ 1))
    middle = make(lambda d, c: (d, 3 - c) if c in (1, 2) else None)
    outward = make(lambda d, c: (d, {1: 0, 2: 3}[c]) if c in (1, 2) else None)
    first = send(own, pair)
    second = send(own, middle)
    shards = {0: part}
    for k in range(2, dp, 2):
        shards[k] = send(part, make(lambda d, c: (d ^ k, c)))
    for k in range(0, dp, 2):
        shards[k + 1] = send(shards[k], make(lambda d, c: (d ^ 1, c)))
    shards = [shards[k] for k in range(dp)]
    third = send(first, middle)
    fourth = send(second, outward)
    fifth = send(third, outward)

    spec = {
        "shards": dp,
        "rows": rows,
        "cols": cols,
        "total": ctx,
        "me": lambda: lax.axis_index("ctx"),
        "owners": lambda: [lax.axis_index("dp") ^ k for k in range(dp)],
        "inner": lambda: jnp.logical_or(lax.axis_index("ctx") == 1, lax.axis_index("ctx") == 2),
    }

    def places():
        c = lax.axis_index("ctx")
        inner = jnp.logical_or(c == 1, c == 2)
        return [c, c ^ 1, c ^ jnp.where(inner, 3, 2), c ^ jnp.where(inner, 2, 3)]

    spec["places"] = places
    inner = spec["inner"]()
    third_block = jnp.where(inner, second, fourth)
    cosine, sine = tables(ctx * rows)
    gain = norm_gain[None, :]
    any_space = pl.BlockSpec(memory_space=pl.ANY)
    vmem = pl.BlockSpec(memory_space=pltpu.VMEM)
    n = 3
    early = pl.pallas_call(
        functools.partial(early_kernel, {**spec, "blocks": n}),
        out_shape=jax.ShapeDtypeStruct((n * rows, 3 * cols), jnp.bfloat16),
        in_specs=[any_space] * (n + dp) + [vmem] * 3,
        out_specs=vmem,
        scratch_shapes=[
            pltpu.VMEM((n * rows, features), jnp.bfloat16),
            pltpu.VMEM((n * rows, features), jnp.bfloat16),
            pltpu.VMEM((features, 3 * cols), jnp.bfloat16),
            pltpu.SemaphoreType.DMA((n,)),
            pltpu.SemaphoreType.DMA((dp,)),
        ],
        compiler_params=pltpu.CompilerParams(vmem_limit_bytes=VMEM_LIMIT),
        cost_estimate=pl.CostEstimate(
            flops=2 * n * rows * features * 3 * cols, bytes_accessed=10_000_000, transcendentals=0
        ),
        name="project_early",
    )(own, first, third_block, *shards, gain, cosine, sine)
    pieces = pl.pallas_call(
        functools.partial(late_kernel, {**spec, "blocks": n}),
        out_shape=[jax.ShapeDtypeStruct((rows, cols), jnp.bfloat16)] * ctx,
        in_specs=[any_space] * (2 + dp + 1) + [vmem] * 3,
        out_specs=[any_space] * ctx,
        scratch_shapes=[
            pltpu.VMEM((rows, features), jnp.bfloat16),
            pltpu.VMEM((rows, features), jnp.bfloat16),
            pltpu.VMEM((features, 3 * cols), jnp.bfloat16),
            pltpu.VMEM((ctx * rows, 3 * cols), jnp.bfloat16),
            pltpu.VMEM((ctx, rows, cols), jnp.bfloat16),
            pltpu.SemaphoreType.DMA((1,)),
            pltpu.SemaphoreType.DMA((dp,)),
            pltpu.SemaphoreType.DMA((n,)),
            pltpu.SemaphoreType.DMA((ctx,)),
        ],
        compiler_params=pltpu.CompilerParams(vmem_limit_bytes=VMEM_LIMIT),
        cost_estimate=pl.CostEstimate(
            flops=2 * rows * features * 3 * cols * 2, bytes_accessed=10_000_000, transcendentals=2_000_000
        ),
        name="attend",
    )(third, fifth, *shards, early, gain, cosine, sine)
    arrived = [pieces[0]]
    for k in range(1, ctx):
        arrived.append(send(pieces[k], make(lambda d, c: (d, c ^ k))))
    return pl.pallas_call(
        functools.partial(join_kernel, spec),
        out_shape=jax.ShapeDtypeStruct((1, rows, ctx * cols), jnp.bfloat16),
        in_specs=[any_space] * ctx,
        out_specs=any_space,
        scratch_shapes=[pltpu.SemaphoreType.DMA((ctx,))],
        compiler_params=pltpu.CompilerParams(vmem_limit_bytes=VMEM_LIMIT),
        name="join",
    )(*arrived)


def rotate(values, positions):
    heads = values.shape[1] // HEAD_DIM
    shaped = values.reshape(values.shape[0], heads, HEAD_DIM)
    freqs = 10000.0 ** (-(jnp.arange(HALF).astype(jnp.float32) * 2.0) / HEAD_DIM)
    angles = positions[:, None] * freqs[None, :]
    cosine = jnp.cos(angles)[:, None, :]
    sine = jnp.sin(angles)[:, None, :]
    first = shaped[:, :, :HALF]
    second = shaped[:, :, HALF:]
    return jnp.concatenate(
        [first * cosine - second * sine, second * cosine + first * sine], axis=2
    )


def general(dp, ctx, tokens, norm_gain, q_weight, k_weight, v_weight):
    rows = tokens.shape[1]
    heads = HEADS // ctx
    cols = heads * HEAD_DIM
    me = lax.axis_index("ctx")
    part = jnp.concatenate(
        [lax.dynamic_slice_in_dim(w, me * cols, cols, 1) for w in (q_weight, k_weight, v_weight)], axis=1
    )
    weights = lax.all_gather(part, "dp", axis=0, tiled=True)
    whole = lax.all_gather(tokens[0], "ctx", axis=0, tiled=True)
    normed = normalize(whole, norm_gain[None, :])
    linear = jnp.dot(normed, weights, preferred_element_type=jnp.float32)
    length = ctx * rows
    positions = jnp.arange(length).astype(jnp.float32)
    q = rotate(linear[:, :cols], positions).astype(jnp.bfloat16)
    k = rotate(linear[:, cols : 2 * cols], positions).astype(jnp.bfloat16)
    v = linear[:, 2 * cols :].astype(jnp.bfloat16).reshape(length, heads, HEAD_DIM)
    allowed = jnp.arange(length)[None, :] <= jnp.arange(length)[:, None]
    scores = jnp.einsum("qhd,khd->hqk", q, k, preferred_element_type=jnp.float32) * HEAD_DIM ** (-0.5)
    scores = jnp.where(allowed[None], scores, -1e30)
    top = jnp.max(scores, axis=2, keepdims=True)
    expo = jnp.where(allowed[None], jnp.exp(scores - top), 0.0)
    numer = jnp.einsum("hqk,khd->hqd", expo.astype(jnp.bfloat16), v, preferred_element_type=jnp.float32)
    result = (numer / jnp.sum(expo, axis=2, keepdims=True)).astype(jnp.bfloat16)
    result = result.reshape(heads, ctx, rows, HEAD_DIM).transpose(1, 2, 0, 3).reshape(ctx, rows, cols)
    back = lax.all_to_all(result, "ctx", 0, 0)
    return back.transpose(1, 0, 2).reshape(1, rows, ctx * cols)


def solution(mesh):
    dp, ctx = mesh.shape["dp"], mesh.shape["ctx"]
    body = fast if (dp, ctx) == (8, 4) else general
    placed = (P("dp", "ctx", None), P(), P("dp", None), P("dp", None), P("dp", None))
    return jax.shard_map(
        functools.partial(body, dp, ctx),
        mesh=mesh,
        in_specs=placed,
        out_specs=P("dp", "ctx", None),
        check_vma=False,
    )
```

```python
import functools
import math

import jax
import jax.numpy as jnp
from jax import lax
from jax.experimental import pallas as pl
from jax.experimental.pallas import tpu as pltpu
from jax.sharding import PartitionSpec as P

HEADS = 16
HEAD_DIM = 128
HALF = HEAD_DIM // 2
EPS = 1e-05
VMEM_LIMIT = 28 * 1024 * 1024


def tables(length):
    freqs = 10000.0 ** (-(jnp.arange(HALF).astype(jnp.float32) * 2.0) / HEAD_DIM)
    angles = jnp.arange(length).astype(jnp.float32)[:, None] * freqs[None, :]
    cosine = jnp.cos(angles)
    sine = jnp.sin(angles)
    return (
        jnp.concatenate([cosine, cosine], axis=1),
        jnp.concatenate([-sine, sine], axis=1),
    )


def normalize(block, gain):
    rows = block.astype(jnp.float32)
    scale = lax.rsqrt(jnp.mean(rows * rows, axis=1, keepdims=True) + EPS)
    return (rows * scale * gain.astype(jnp.float32)).astype(jnp.bfloat16)


def project(normed, weights, cos_ref, sin_ref, starts, rows, cols, store):
    step = 2 * HEAD_DIM
    for first in range(0, 3 * cols, step):
        linear = jnp.dot(
            normed[...], weights[:, first : first + step], preferred_element_type=jnp.float32
        )
        for block, start in enumerate(starts):
            part = linear[block * rows : (block + 1) * rows]
            if first < 2 * cols:
                cosine = cos_ref[pl.ds(start, rows), :]
                sine = sin_ref[pl.ds(start, rows), :]
                heads = [part[:, h * HEAD_DIM : (h + 1) * HEAD_DIM] for h in range(2)]
                part = jnp.concatenate(
                    [x * cosine + pltpu.roll(x, HALF, 1) * sine for x in heads], axis=1
                )
            store(block, first, step, part.astype(jnp.bfloat16))


def start_weights(owners, shards, weights, sems):
    depth = shards[0].shape[0]
    copies = []
    for i, (owner, shard) in enumerate(zip(owners, shards)):
        copy = pltpu.make_async_copy(
            shard, weights.at[pl.ds(pl.multiple_of(owner * depth, depth), depth)], sems.at[i]
        )
        copy.start()
        copies.append(copy)
    return copies


def early_kernel(spec, *refs):
    n, m, rows, cols = spec["blocks"], spec["shards"], spec["rows"], spec["cols"]
    tokens, shards = refs[: n + 1], refs[n + 1 : n + 1 + m]
    gain, cos_ref, sin_ref, out, held, normed, weights, token_sems, weight_sems = refs[n + 1 + m :]
    place, owners = spec["places"](), spec["owners"]()
    inner = spec["inner"]()
    loads = []
    for i in range(n):
        load = pltpu.make_async_copy(
            tokens[i], held.at[pl.ds(i * rows, rows)], token_sems.at[i]
        )
        loads.append(load)
        if i < n - 1:
            load.start()
        else:
            pl.when(inner)(load.start)
            other = pltpu.make_async_copy(
                tokens[n], held.at[pl.ds(i * rows, rows)], token_sems.at[i]
            )
            pl.when(jnp.logical_not(inner))(other.start)
    weight_loads = start_weights(owners, shards, weights, weight_sems)
    for i in range(n):
        loads[i].wait()
        part = pl.ds(i * rows, rows)
        normed[part, :] = normalize(held[part, :], gain[...])
    for load in weight_loads:
        load.wait()
    starts = [pl.multiple_of(place[i] * rows, rows) for i in range(n)]

    def store(block, first, step, value):
        out[pl.ds(block * rows, rows), pl.ds(first, step)] = value

    project(normed, weights, cos_ref, sin_ref, starts, rows, cols, store)


def late_kernel(spec, *refs):
    n, m, rows, cols = spec["blocks"], spec["shards"], spec["rows"], spec["cols"]
    total = spec["total"]
    tokens, shards = refs[:2], refs[2 : 2 + m]
    early, gain, cos_ref, sin_ref = refs[2 + m : 6 + m]
    outs = refs[6 + m : 6 + m + total]
    held, normed, weights, qkv, result, token_sems, weight_sems, early_sems, out_sems = refs[6 + m + total :]
    place, owners = spec["places"](), spec["owners"]()
    me = spec["me"]()
    inner = spec["inner"]()
    weight_loads = start_weights(owners, shards, weights, weight_sems)

    @pl.when(inner)
    def _():
        pltpu.make_async_copy(tokens[0], held, token_sems.at[0]).start()

    @pl.when(jnp.logical_not(inner))
    def _():
        pltpu.make_async_copy(tokens[1], held, token_sems.at[0]).start()

    early_loads = []
    for i in range(n):
        load = pltpu.make_async_copy(
            early.at[pl.ds(i * rows, rows)],
            qkv.at[pl.ds(pl.multiple_of(place[i] * rows, rows), rows)],
            early_sems.at[i],
        )
        load.start()
        early_loads.append(load)
    pltpu.make_async_copy(tokens[0], held, token_sems.at[0]).wait()
    normed[...] = normalize(held[...], gain[...])
    for load in weight_loads:
        load.wait()
    last = pl.multiple_of(place[n] * rows, rows)

    def store(block, first, step, value):
        qkv[pl.ds(last, rows), pl.ds(first, step)] = value

    project(normed, weights, cos_ref, sin_ref, [last], rows, cols, store)
    for load in early_loads:
        load.wait()
    attend(qkv, result, me, total, rows, cols)
    copies = []
    for k in range(total):
        copy = pltpu.make_async_copy(result.at[k], outs[k], out_sems.at[k])
        copy.start()
        copies.append(copy)
    for copy in copies:
        copy.wait()


def attend(qkv, result, me, total, rows, cols):
    factor = HEAD_DIM ** (-0.5) * math.log2(math.e)
    below = lax.broadcasted_iota(jnp.int32, (rows, rows), 0) >= lax.broadcasted_iota(
        jnp.int32, (rows, rows), 1
    )

    def scored(q, k):
        return lax.dot_general(q, k, (((1,), (1,)), ((), ())), preferred_element_type=jnp.float32)

    for block in range(total):
        own, past = slice(block * rows, (block + 1) * rows), slice(0, block * rows)
        for head in range(cols // HEAD_DIM):
            lane = slice(head * HEAD_DIM, (head + 1) * HEAD_DIM)
            k_lane = slice(cols + lane.start, cols + lane.stop)
            v_lane = slice(2 * cols + lane.start, 2 * cols + lane.stop)
            q = qkv[own, lane]
            near = jnp.where(below, scored(q, qkv[own, k_lane]), -1e30)
            top = jnp.max(near, axis=1, keepdims=True)
            if block:
                far = scored(q, qkv[past, k_lane])
                top = jnp.maximum(top, jnp.max(far, axis=1, keepdims=True))
            top = top * factor
            expo = jnp.exp2(near * factor - top)
            bottom = jnp.sum(expo, axis=1, keepdims=True)
            numer = jnp.dot(expo.astype(jnp.bfloat16), qkv[own, v_lane], preferred_element_type=jnp.float32)
            if block:
                expo = jnp.exp2(far * factor - top)
                bottom += jnp.sum(expo, axis=1, keepdims=True)
                numer += jnp.dot(
                    expo.astype(jnp.bfloat16), qkv[past, v_lane], preferred_element_type=jnp.float32
                )
            result[block ^ me, :, lane] = (numer / bottom).astype(jnp.bfloat16)


def join_kernel(spec, *refs):
    total, cols = spec["total"], spec["cols"]
    me = spec["me"]()
    for k in range(total):
        refs[total][0, :, pl.ds(pl.multiple_of((me ^ k) * cols, cols), cols)] = refs[k][...]


def block_plan(dp, ctx):
    flat = lambda d, c: d * ctx + c
    every = [(d, c) for d in range(dp) for c in range(ctx)]
    make = lambda to: [
        (flat(d, c), flat(*to(d, c))) for d, c in every if to(d, c) is not None
    ]
    return make


def fast(dp, ctx, tokens, norm_gain, q_weight, k_weight, v_weight):
    rows, features = tokens.shape[1], tokens.shape[2]
    depth = q_weight.shape[0]
    cols = HEADS // ctx * HEAD_DIM
    make = block_plan(dp, ctx)
    axes = ("dp", "ctx")
    send = lambda value, perm: lax.ppermute(value, axes, perm)
    me = lax.axis_index("ctx")
    own = tokens[0]
    part = jnp.concatenate(
        [lax.dynamic_slice_in_dim(w, me * cols, cols, 1) for w in (q_weight, k_weight, v_weight)], axis=1
    )
    pair = make(lambda d, c: (d, c ^ 1))
    middle = make(lambda d, c: (d, 3 - c) if c in (1, 2) else None)
    outward = make(lambda d, c: (d, {1: 0, 2: 3}[c]) if c in (1, 2) else None)
    first = send(own, pair)
    second = send(own, middle)
    cosine, sine = tables(ctx * rows)
    first, cosine, sine = lax.optimization_barrier((first, cosine, sine))
    shards = {0: part}
    for k in range(2, dp, 2):
        shards[k] = send(part, make(lambda d, c: (d ^ k, c)))
    for k in range(0, dp, 2):
        shards[k + 1] = send(shards[k], make(lambda d, c: (d ^ 1, c)))
    shards = [shards[k] for k in range(dp)]
    third = send(first, middle)
    fourth = send(second, outward)
    fifth = send(third, outward)

    spec = {
        "shards": dp,
        "rows": rows,
        "cols": cols,
        "total": ctx,
        "me": lambda: lax.axis_index("ctx"),
        "owners": lambda: [lax.axis_index("dp") ^ k for k in range(dp)],
        "inner": lambda: jnp.logical_or(lax.axis_index("ctx") == 1, lax.axis_index("ctx") == 2),
    }

    def places():
        c = lax.axis_index("ctx")
        inner = jnp.logical_or(c == 1, c == 2)
        return [c, c ^ 1, c ^ jnp.where(inner, 3, 2), c ^ jnp.where(inner, 2, 3)]

    spec["places"] = places
    gain = norm_gain[None, :]
    any_space = pl.BlockSpec(memory_space=pl.ANY)
    vmem = pl.BlockSpec(memory_space=pltpu.VMEM)
    n = 3
    early = pl.pallas_call(
        functools.partial(early_kernel, {**spec, "blocks": n}),
        out_shape=jax.ShapeDtypeStruct((n * rows, 3 * cols), jnp.bfloat16),
        in_specs=[any_space] * (n + 1 + dp) + [vmem] * 3,
        out_specs=vmem,
        scratch_shapes=[
            pltpu.VMEM((n * rows, features), jnp.bfloat16),
            pltpu.VMEM((n * rows, features), jnp.bfloat16),
            pltpu.VMEM((features, 3 * cols), jnp.bfloat16),
            pltpu.SemaphoreType.DMA((n,)),
            pltpu.SemaphoreType.DMA((dp,)),
        ],
        compiler_params=pltpu.CompilerParams(vmem_limit_bytes=VMEM_LIMIT),
        cost_estimate=pl.CostEstimate(
            flops=2 * n * rows * features * 3 * cols, bytes_accessed=10_000_000, transcendentals=0
        ),
        name="project_early",
    )(own, first, second, fourth, *shards, gain, cosine, sine)
    pieces = pl.pallas_call(
        functools.partial(late_kernel, {**spec, "blocks": n}),
        out_shape=[jax.ShapeDtypeStruct((rows, cols), jnp.bfloat16)] * ctx,
        in_specs=[any_space] * (2 + dp + 1) + [vmem] * 3,
        out_specs=[any_space] * ctx,
        scratch_shapes=[
            pltpu.VMEM((rows, features), jnp.bfloat16),
            pltpu.VMEM((rows, features), jnp.bfloat16),
            pltpu.VMEM((features, 3 * cols), jnp.bfloat16),
            pltpu.VMEM((ctx * rows, 3 * cols), jnp.bfloat16),
            pltpu.VMEM((ctx, rows, cols), jnp.bfloat16),
            pltpu.SemaphoreType.DMA((1,)),
            pltpu.SemaphoreType.DMA((dp,)),
            pltpu.SemaphoreType.DMA((n,)),
            pltpu.SemaphoreType.DMA((ctx,)),
        ],
        compiler_params=pltpu.CompilerParams(vmem_limit_bytes=VMEM_LIMIT),
        cost_estimate=pl.CostEstimate(
            flops=2 * rows * features * 3 * cols * 2, bytes_accessed=10_000_000, transcendentals=2_000_000
        ),
        name="attend",
    )(third, fifth, *shards, early, gain, cosine, sine)
    arrived = [pieces[0]]
    for k in range(1, ctx):
        arrived.append(send(pieces[k], make(lambda d, c: (d, c ^ k))))
    return pl.pallas_call(
        functools.partial(join_kernel, spec),
        out_shape=jax.ShapeDtypeStruct((1, rows, ctx * cols), jnp.bfloat16),
        in_specs=[vmem] * ctx,
        out_specs=vmem,
        compiler_params=pltpu.CompilerParams(vmem_limit_bytes=8 * 1024 * 1024),
        name="join",
    )(*arrived)


def rotate(values, positions):
    heads = values.shape[1] // HEAD_DIM
    shaped = values.reshape(values.shape[0], heads, HEAD_DIM)
    freqs = 10000.0 ** (-(jnp.arange(HALF).astype(jnp.float32) * 2.0) / HEAD_DIM)
    angles = positions[:, None] * freqs[None, :]
    cosine = jnp.cos(angles)[:, None, :]
    sine = jnp.sin(angles)[:, None, :]
    first = shaped[:, :, :HALF]
    second = shaped[:, :, HALF:]
    return jnp.concatenate(
        [first * cosine - second * sine, second * cosine + first * sine], axis=2
    )


def general(dp, ctx, tokens, norm_gain, q_weight, k_weight, v_weight):
    rows = tokens.shape[1]
    heads = HEADS // ctx
    cols = heads * HEAD_DIM
    me = lax.axis_index("ctx")
    part = jnp.concatenate(
        [lax.dynamic_slice_in_dim(w, me * cols, cols, 1) for w in (q_weight, k_weight, v_weight)], axis=1
    )
    weights = lax.all_gather(part, "dp", axis=0, tiled=True)
    whole = lax.all_gather(tokens[0], "ctx", axis=0, tiled=True)
    normed = normalize(whole, norm_gain[None, :])
    linear = jnp.dot(normed, weights, preferred_element_type=jnp.float32)
    length = ctx * rows
    positions = jnp.arange(length).astype(jnp.float32)
    q = rotate(linear[:, :cols], positions).astype(jnp.bfloat16)
    k = rotate(linear[:, cols : 2 * cols], positions).astype(jnp.bfloat16)
    v = linear[:, 2 * cols :].astype(jnp.bfloat16).reshape(length, heads, HEAD_DIM)
    allowed = jnp.arange(length)[None, :] <= jnp.arange(length)[:, None]
    scores = jnp.einsum("qhd,khd->hqk", q, k, preferred_element_type=jnp.float32) * HEAD_DIM ** (-0.5)
    scores = jnp.where(allowed[None], scores, -1e30)
    top = jnp.max(scores, axis=2, keepdims=True)
    expo = jnp.where(allowed[None], jnp.exp(scores - top), 0.0)
    numer = jnp.einsum("hqk,khd->hqd", expo.astype(jnp.bfloat16), v, preferred_element_type=jnp.float32)
    result = (numer / jnp.sum(expo, axis=2, keepdims=True)).astype(jnp.bfloat16)
    result = result.reshape(heads, ctx, rows, HEAD_DIM).transpose(1, 2, 0, 3).reshape(ctx, rows, cols)
    back = lax.all_to_all(result, "ctx", 0, 0)
    return back.transpose(1, 0, 2).reshape(1, rows, ctx * cols)


def solution(mesh):
    dp, ctx = mesh.shape["dp"], mesh.shape["ctx"]
    body = fast if (dp, ctx) == (8, 4) else general
    placed = (P("dp", "ctx", None), P(), P("dp", None), P("dp", None), P("dp", None))
    return jax.shard_map(
        functools.partial(body, dp, ctx),
        mesh=mesh,
        in_specs=placed,
        out_specs=P("dp", "ctx", None),
        check_vma=False,
    )
```

```python
import functools
import math

import jax
import jax.numpy as jnp
from jax import lax
from jax.experimental import pallas as pl
from jax.experimental.pallas import tpu as pltpu
from jax.sharding import PartitionSpec as P

HEADS = 16
HEAD_DIM = 128
HALF = HEAD_DIM // 2
EPS = 1e-05
VMEM_LIMIT = 28 * 1024 * 1024


def tables(length):
    freqs = 10000.0 ** (-(jnp.arange(HALF).astype(jnp.float32) * 2.0) / HEAD_DIM)
    angles = jnp.arange(length).astype(jnp.float32)[:, None] * freqs[None, :]
    cosine = jnp.cos(angles)
    sine = jnp.sin(angles)
    return (
        jnp.concatenate([cosine, cosine], axis=1),
        jnp.concatenate([-sine, sine], axis=1),
    )


def normalize(block, gain):
    rows = block.astype(jnp.float32)
    scale = lax.rsqrt(jnp.mean(rows * rows, axis=1, keepdims=True) + EPS)
    return (rows * scale * gain.astype(jnp.float32)).astype(jnp.bfloat16)


def project(normed, weights, cos_ref, sin_ref, parts, cols, store):
    step = 2 * HEAD_DIM
    for first in range(0, 3 * cols, step):
        linear = jnp.dot(
            normed[...], weights[:, first : first + step], preferred_element_type=jnp.float32
        )
        for row, rows, start in parts:
            part = linear[row : row + rows]
            if first < 2 * cols:
                cosine = cos_ref[pl.ds(start, rows), :]
                sine = sin_ref[pl.ds(start, rows), :]
                heads = [part[:, h * HEAD_DIM : (h + 1) * HEAD_DIM] for h in range(2)]
                part = jnp.concatenate(
                    [x * cosine + pltpu.roll(x, HALF, 1) * sine for x in heads], axis=1
                )
            store(row, rows, start, first, step, part.astype(jnp.bfloat16))


def start_weights(owners, shards, weights, sems):
    depth = shards[0].shape[0]
    copies = []
    for i, (owner, shard) in enumerate(zip(owners, shards)):
        copy = pltpu.make_async_copy(
            shard, weights.at[pl.ds(pl.multiple_of(owner * depth, depth), depth)], sems.at[i]
        )
        copy.start()
        copies.append(copy)
    return copies


def role(rows):
    d, c = lax.axis_index("dp"), lax.axis_index("ctx")
    y, core = d // 4, d % 2
    lone = core == 0
    inner = jnp.logical_or(c == 1, c == 2)
    home = c // 2 == y
    half = rows // 2
    near = c ^ jnp.where(inner, 3, 2)
    far = c ^ jnp.where(inner, 2, 3)
    mine, other = y * half, (1 - y) * half
    hint = lambda value: pl.multiple_of(value, half)
    early = [
        (0, rows, hint(c * rows)),
        (rows, rows, hint((c ^ 1) * rows)),
        (2 * rows, half, hint(jnp.where(lone, near * rows, (c ^ 2) * rows + mine))),
        (2 * rows + half, half, hint(jnp.where(lone, near * rows + half, (c ^ 3) * rows + mine))),
    ]
    late = [
        (0, half, hint(jnp.where(lone, far * rows, (c ^ 2) * rows + other))),
        (half, half, hint(jnp.where(lone, far * rows + half, (c ^ 3) * rows + other))),
    ]
    return {
        "lone": lone,
        "inner": inner,
        "home": home,
        "mine": hint(mine),
        "other": hint(other),
        "early": early,
        "late": late,
        "base": jnp.where(lone, c, 2 * y + c % 2),
        "owners": [d ^ k for k in range(8)],
    }


def begin(cases):
    for condition, copies in cases:

        @pl.when(condition)
        def _(copies=copies):
            for source, target, sem in copies:
                pltpu.make_async_copy(source, target, sem).start()


def early_kernel(rows, cols, *refs):
    own, first, second, fourth, swap0, swap1, r1, r2, r3, x1 = refs[:10]
    shards = refs[10:18]
    gain, cos_ref, sin_ref, out, held, normed, weights, token_sems, weight_sems = refs[18:]
    me = role(rows)
    half = rows // 2
    slot = lambda i: held.at[pl.ds(i * rows, rows)]
    part = lambda i, start: held.at[pl.ds(i * rows + start, half)]
    sems = [token_sems.at[i] for i in range(3)]
    mine, other = me["mine"], me["other"]
    both = jnp.logical_and
    paired = jnp.logical_not(me["lone"])
    away = jnp.logical_not(me["home"])
    begin(
        [
            (jnp.logical_or(me["lone"], me["home"]), [(own, slot(0), sems[0])]),
            (
                both(paired, away),
                [(swap0, part(0, mine), sems[0]), (swap1, part(0, other), sems[0])],
            ),
            (me["lone"], [(first, slot(1), sems[1])]),
            (paired, [(r1, part(1, mine), sems[1]), (x1, part(1, other), sems[1])]),
            (both(me["lone"], me["inner"]), [(second, slot(2), sems[2])]),
            (both(me["lone"], jnp.logical_not(me["inner"])), [(fourth, slot(2), sems[2])]),
            (paired, [(r2, part(2, 0), sems[2]), (r3, part(2, half), sems[2])]),
        ]
    )
    weight_loads = start_weights(me["owners"], shards, weights, weight_sems)
    for i in range(3):
        pltpu.make_async_copy(own, slot(i), sems[i]).wait()
        normed[pl.ds(i * rows, rows), :] = normalize(slot(i)[...], gain[...])
    for load in weight_loads:
        load.wait()

    def store(row, count, start, lane, step, value):
        out[pl.ds(row, count), pl.ds(lane, step)] = value

    project(normed, weights, cos_ref, sin_ref, me["early"], cols, store)


def late_kernel(rows, cols, total, *refs):
    third, fifth, x2, x3 = refs[:4]
    shards = refs[4:12]
    early, gain, cos_ref, sin_ref = refs[12:16]
    outs = refs[16 : 16 + total]
    held, normed, weights, qkv, result, token_sem, weight_sems, early_sems, out_sems = refs[16 + total :]
    me = role(rows)
    half = rows // 2
    paired = jnp.logical_not(me["lone"])
    begin(
        [
            (jnp.logical_and(me["lone"], me["inner"]), [(third, held, token_sem)]),
            (jnp.logical_and(me["lone"], jnp.logical_not(me["inner"])), [(fifth, held, token_sem)]),
            (
                paired,
                [
                    (x2, held.at[pl.ds(0, half)], token_sem),
                    (x3, held.at[pl.ds(half, half)], token_sem),
                ],
            ),
        ]
    )
    weight_loads = start_weights(me["owners"], shards, weights, weight_sems)
    early_loads = []
    for i, (row, count, start) in enumerate(me["early"]):
        load = pltpu.make_async_copy(
            early.at[pl.ds(row, count)], qkv.at[pl.ds(start, count)], early_sems.at[i]
        )
        load.start()
        early_loads.append(load)
    pltpu.make_async_copy(third, held, token_sem).wait()
    normed[...] = normalize(held[...], gain[...])
    for load in weight_loads:
        load.wait()

    def store(row, count, start, lane, step, value):
        qkv[pl.ds(start, count), pl.ds(lane, step)] = value

    project(normed, weights, cos_ref, sin_ref, me["late"], cols, store)
    for load in early_loads:
        load.wait()
    attend(qkv, result, me["base"], total, rows, cols)
    copies = []
    for k in range(total):
        copy = pltpu.make_async_copy(result.at[k], outs[k], out_sems.at[k])
        copy.start()
        copies.append(copy)
    for copy in copies:
        copy.wait()


def attend(qkv, result, me, total, rows, cols):
    factor = HEAD_DIM ** (-0.5) * math.log2(math.e)
    below = lax.broadcasted_iota(jnp.int32, (rows, rows), 0) >= lax.broadcasted_iota(
        jnp.int32, (rows, rows), 1
    )

    def scored(q, k):
        return lax.dot_general(q, k, (((1,), (1,)), ((), ())), preferred_element_type=jnp.float32)

    for block in range(total):
        own, past = slice(block * rows, (block + 1) * rows), slice(0, block * rows)
        for head in range(cols // HEAD_DIM):
            lane = slice(head * HEAD_DIM, (head + 1) * HEAD_DIM)
            k_lane = slice(cols + lane.start, cols + lane.stop)
            v_lane = slice(2 * cols + lane.start, 2 * cols + lane.stop)
            q = qkv[own, lane]
            near = jnp.where(below, scored(q, qkv[own, k_lane]), -1e30)
            top = jnp.max(near, axis=1, keepdims=True)
            if block:
                far = scored(q, qkv[past, k_lane])
                top = jnp.maximum(top, jnp.max(far, axis=1, keepdims=True))
            top = top * factor
            expo = jnp.exp2(near * factor - top)
            bottom = jnp.sum(expo, axis=1, keepdims=True)
            numer = jnp.dot(expo.astype(jnp.bfloat16), qkv[own, v_lane], preferred_element_type=jnp.float32)
            if block:
                expo = jnp.exp2(far * factor - top)
                bottom += jnp.sum(expo, axis=1, keepdims=True)
                numer += jnp.dot(
                    expo.astype(jnp.bfloat16), qkv[past, v_lane], preferred_element_type=jnp.float32
                )
            result[block ^ me, :, lane] = (numer / bottom).astype(jnp.bfloat16)


def join_kernel(cols, total, own, *refs):
    pieces, out = refs[:total], refs[total]
    d, c = lax.axis_index("dp"), lax.axis_index("ctx")
    y, lone = d // 4, d % 2 == 0
    for k in range(total):
        source = c ^ k
        heads = jnp.where(lone, source ^ (2 * y), (2 * y + source % 2) ^ (2 * (source // 2)))
        lane = pl.ds(pl.multiple_of(heads * cols, cols), cols)
        if k:
            out[0, :, lane] = pieces[k][...]
        else:
            kept = jnp.logical_or(lone, c // 2 == y)
            out[0, :, lane] = jnp.where(kept, own[...], pieces[k][...])


def fast(dp, ctx, tokens, norm_gain, q_weight, k_weight, v_weight):
    rows, features = tokens.shape[1], tokens.shape[2]
    half = rows // 2
    cols = HEADS // ctx * HEAD_DIM
    every = [(d, c) for d in range(dp) for c in range(ctx)]

    def send(value, to):
        perm = [
            (d * ctx + c, to(d, c)[0] * ctx + to(d, c)[1]) for d, c in every if to(d, c) is not None
        ]
        return lax.ppermute(value, ("dp", "ctx"), perm)

    def lone(to):
        return lambda d, c: None if d & 1 else to(d, c)

    def paired(to):
        return lambda d, c: to(d, c) if d & 1 else None

    pair = lone(lambda d, c: (d, c ^ 1))
    middle = lone(lambda d, c: (d, 3 - c) if c in (1, 2) else None)
    outward = lone(lambda d, c: (d, {1: 0, 2: 3}[c]) if c in (1, 2) else None)
    across = paired(lambda d, c: (d ^ 4, c))
    d, c = lax.axis_index("dp"), lax.axis_index("ctx")
    y = d // 4
    own = tokens[0]
    mine = lax.dynamic_slice_in_dim(own, y * half, half, 0)
    other = lax.dynamic_slice_in_dim(own, (1 - y) * half, half, 0)
    first = send(own, pair)
    second = send(own, middle)
    swap0 = send(other, across)

    def columns(heads):
        return jnp.concatenate(
            [lax.dynamic_slice_in_dim(w, heads * cols, cols, 1) for w in (q_weight, k_weight, v_weight)],
            axis=1,
        )

    heads = c ^ (2 * y)
    shards = {0: columns(heads)}
    shards[2] = send(shards[0], lambda d, c: (d ^ 2, c))
    shards[4] = send(columns(heads ^ 2), lambda d, c: (d ^ 4, c))
    swap1 = send(mine, paired(lambda d, c: (d ^ 4, c) if c // 2 == d >> 2 else None))
    cosine, sine = tables(ctx * rows)
    first, cosine, sine = lax.optimization_barrier((first, cosine, sine))
    third = send(first, middle)
    fourth = send(second, outward)
    home = c // 2 == y
    r1 = send(jnp.where(home, mine, swap0), paired(lambda d, c: (d, c ^ 1)))
    cross = jnp.where(home, swap0, mine)
    r2 = send(cross, paired(lambda d, c: (d, c ^ 2)))
    r3 = send(cross, paired(lambda d, c: (d, c ^ 3)))
    shards[6] = send(shards[4], lambda d, c: (d ^ 2, c))
    x1 = send(r1, across)
    x2 = send(r2, across)
    x3 = send(r3, across)
    fifth = send(third, outward)
    for k in range(0, dp, 2):
        shards[k + 1] = send(shards[k], lambda d, c: (d ^ 1, c))
    shards = [shards[k] for k in range(dp)]

    gain = norm_gain[None, :]
    any_space = pl.BlockSpec(memory_space=pl.ANY)
    vmem = pl.BlockSpec(memory_space=pltpu.VMEM)
    early = pl.pallas_call(
        functools.partial(early_kernel, rows, cols),
        out_shape=jax.ShapeDtypeStruct((3 * rows, 3 * cols), jnp.bfloat16),
        in_specs=[any_space] * 18 + [vmem] * 3,
        out_specs=vmem,
        scratch_shapes=[
            pltpu.VMEM((3 * rows, features), jnp.bfloat16),
            pltpu.VMEM((3 * rows, features), jnp.bfloat16),
            pltpu.VMEM((features, 3 * cols), jnp.bfloat16),
            pltpu.SemaphoreType.DMA((3,)),
            pltpu.SemaphoreType.DMA((dp,)),
        ],
        compiler_params=pltpu.CompilerParams(vmem_limit_bytes=VMEM_LIMIT),
        cost_estimate=pl.CostEstimate(
            flops=2 * 3 * rows * features * 3 * cols, bytes_accessed=10_000_000, transcendentals=0
        ),
        name="project_early",
    )(own, first, second, fourth, swap0, swap1, r1, r2, r3, x1, *shards, gain, cosine, sine)
    pieces = pl.pallas_call(
        functools.partial(late_kernel, rows, cols, ctx),
        out_shape=[jax.ShapeDtypeStruct((rows, cols), jnp.bfloat16)] * ctx,
        in_specs=[any_space] * 13 + [vmem] * 3,
        out_specs=[any_space] * ctx,
        scratch_shapes=[
            pltpu.VMEM((rows, features), jnp.bfloat16),
            pltpu.VMEM((rows, features), jnp.bfloat16),
            pltpu.VMEM((features, 3 * cols), jnp.bfloat16),
            pltpu.VMEM((ctx * rows, 3 * cols), jnp.bfloat16),
            pltpu.VMEM((ctx, rows, cols), jnp.bfloat16),
            pltpu.SemaphoreType.DMA,
            pltpu.SemaphoreType.DMA((dp,)),
            pltpu.SemaphoreType.DMA((4,)),
            pltpu.SemaphoreType.DMA((ctx,)),
        ],
        compiler_params=pltpu.CompilerParams(vmem_limit_bytes=VMEM_LIMIT),
        cost_estimate=pl.CostEstimate(
            flops=2 * rows * features * 3 * cols * 2, bytes_accessed=10_000_000, transcendentals=2_000_000
        ),
        name="attend",
    )(third, fifth, x2, x3, *shards, early, gain, cosine, sine)

    def back(k):
        def to(d, c):
            if d & 1:
                target = ((d & 3) | (c // 2) << 2, (2 * (d >> 2) + c % 2) ^ k)
            else:
                target = (d, c ^ k)
            return None if target == (d, c) else target

        return to

    arrived = [send(pieces[k], back(k)) for k in range(ctx)]
    return pl.pallas_call(
        functools.partial(join_kernel, cols, ctx),
        out_shape=jax.ShapeDtypeStruct((1, rows, ctx * cols), jnp.bfloat16),
        in_specs=[vmem] * (ctx + 1),
        out_specs=vmem,
        compiler_params=pltpu.CompilerParams(vmem_limit_bytes=8 * 1024 * 1024),
        name="join",
    )(pieces[0], *arrived)


def rotate(values, positions):
    heads = values.shape[1] // HEAD_DIM
    shaped = values.reshape(values.shape[0], heads, HEAD_DIM)
    freqs = 10000.0 ** (-(jnp.arange(HALF).astype(jnp.float32) * 2.0) / HEAD_DIM)
    angles = positions[:, None] * freqs[None, :]
    cosine = jnp.cos(angles)[:, None, :]
    sine = jnp.sin(angles)[:, None, :]
    first = shaped[:, :, :HALF]
    second = shaped[:, :, HALF:]
    return jnp.concatenate(
        [first * cosine - second * sine, second * cosine + first * sine], axis=2
    )


def general(dp, ctx, tokens, norm_gain, q_weight, k_weight, v_weight):
    rows = tokens.shape[1]
    heads = HEADS // ctx
    cols = heads * HEAD_DIM
    me = lax.axis_index("ctx")
    part = jnp.concatenate(
        [lax.dynamic_slice_in_dim(w, me * cols, cols, 1) for w in (q_weight, k_weight, v_weight)], axis=1
    )
    weights = lax.all_gather(part, "dp", axis=0, tiled=True)
    whole = lax.all_gather(tokens[0], "ctx", axis=0, tiled=True)
    normed = normalize(whole, norm_gain[None, :])
    linear = jnp.dot(normed, weights, preferred_element_type=jnp.float32)
    length = ctx * rows
    positions = jnp.arange(length).astype(jnp.float32)
    q = rotate(linear[:, :cols], positions).astype(jnp.bfloat16)
    k = rotate(linear[:, cols : 2 * cols], positions).astype(jnp.bfloat16)
    v = linear[:, 2 * cols :].astype(jnp.bfloat16).reshape(length, heads, HEAD_DIM)
    allowed = jnp.arange(length)[None, :] <= jnp.arange(length)[:, None]
    scores = jnp.einsum("qhd,khd->hqk", q, k, preferred_element_type=jnp.float32) * HEAD_DIM ** (-0.5)
    scores = jnp.where(allowed[None], scores, -1e30)
    top = jnp.max(scores, axis=2, keepdims=True)
    expo = jnp.where(allowed[None], jnp.exp(scores - top), 0.0)
    numer = jnp.einsum("hqk,khd->hqd", expo.astype(jnp.bfloat16), v, preferred_element_type=jnp.float32)
    result = (numer / jnp.sum(expo, axis=2, keepdims=True)).astype(jnp.bfloat16)
    result = result.reshape(heads, ctx, rows, HEAD_DIM).transpose(1, 2, 0, 3).reshape(ctx, rows, cols)
    back = lax.all_to_all(result, "ctx", 0, 0)
    return back.transpose(1, 0, 2).reshape(1, rows, ctx * cols)


def solution(mesh):
    dp, ctx = mesh.shape["dp"], mesh.shape["ctx"]
    body = fast if (dp, ctx) == (8, 4) else general
    placed = (P("dp", "ctx", None), P(), P("dp", None), P("dp", None), P("dp", None))
    return jax.shard_map(
        functools.partial(body, dp, ctx),
        mesh=mesh,
        in_specs=placed,
        out_specs=P("dp", "ctx", None),
        check_vma=False,
    )
```

```python
import functools
import math

import jax
import jax.numpy as jnp
from jax import lax
from jax.experimental import pallas as pl
from jax.experimental.pallas import tpu as pltpu
from jax.sharding import PartitionSpec as P

HEADS = 16
HEAD_DIM = 128
HALF = HEAD_DIM // 2
EPS = 1e-05
VMEM_LIMIT = 28 * 1024 * 1024


def tables(length):
    freqs = 10000.0 ** (-(jnp.arange(HALF).astype(jnp.float32) * 2.0) / HEAD_DIM)
    angles = jnp.arange(length).astype(jnp.float32)[:, None] * freqs[None, :]
    cosine = jnp.cos(angles)
    sine = jnp.sin(angles)
    return (
        jnp.concatenate([cosine, cosine], axis=1),
        jnp.concatenate([-sine, sine], axis=1),
    )


def normalize(block, gain):
    rows = block.astype(jnp.float32)
    scale = lax.rsqrt(jnp.mean(rows * rows, axis=1, keepdims=True) + EPS)
    return (rows * scale * gain.astype(jnp.float32)).astype(jnp.bfloat16)


def role(rows):
    d, c = lax.axis_index("dp"), lax.axis_index("ctx")
    home = c // 2 == d % 2
    return {
        "home": home,
        "starts": [pl.multiple_of((c ^ i) * rows, rows) for i in range(4)],
        "base": jnp.where(home, c, c ^ 2),
        "owner": d,
    }


def early_kernel(rows, cols, *refs):
    kept, sent, shards = refs[:4], refs[4:8], refs[8:14]
    gain, out, tail, held, normed, weights, token_sems, weight_sems = refs[14:]
    me = role(rows)
    depth = shards[0].shape[0]
    loads = []
    for i in range(4):
        slot = held.at[pl.ds(i * rows, rows)]
        for condition, source in ((me["home"], kept[i]), (jnp.logical_not(me["home"]), sent[i])):

            @pl.when(condition)
            def _(source=source, slot=slot, i=i):
                pltpu.make_async_copy(source, slot, token_sems.at[i]).start()

        loads.append(pltpu.make_async_copy(kept[i], slot, token_sems.at[i]))
    weight_loads = []
    for i, shard in enumerate(shards):
        load = pltpu.make_async_copy(shard, weights.at[pl.ds(i * depth, depth)], weight_sems.at[i])
        load.start()
        weight_loads.append(load)
    for i in range(4):
        loads[i].wait()
        part = pl.ds(i * rows, rows)
        value = normalize(held[part, :], gain[...])
        for owner in range(8):
            offset = me["owner"] ^ owner
            place = jnp.where(offset < 3, offset, jnp.where(offset < 5, offset + 3, offset - 2))
            lane = pl.ds(pl.multiple_of(place * depth, depth), depth)
            normed[part, lane] = value[:, owner * depth : (owner + 1) * depth]
    for load in weight_loads:
        load.wait()
    first = len(shards) * depth
    tail[...] = normed[:, first:]
    step = 2 * HEAD_DIM
    for lane in range(0, 3 * cols, step):
        out[:, lane : lane + step] = jnp.dot(
            normed[:, :first], weights[:, lane : lane + step], preferred_element_type=jnp.float32
        )


def late_kernel(rows, cols, total, *refs):
    shards = refs[:2]
    partial, tail, cos_ref, sin_ref = refs[2:6]
    outs = refs[6 : 6 + total]
    weights, qkv, result, weight_sems, out_sems = refs[6 + total :]
    me = role(rows)
    depth = shards[0].shape[0]
    loads = []
    for i, shard in enumerate(shards):
        load = pltpu.make_async_copy(shard, weights.at[pl.ds(i * depth, depth)], weight_sems.at[i])
        load.start()
        loads.append(load)
    for load in loads:
        load.wait()
    step = 2 * HEAD_DIM
    for first in range(0, 3 * cols, step):
        linear = partial[:, first : first + step] + jnp.dot(
            tail[...], weights[:, first : first + step], preferred_element_type=jnp.float32
        )
        for i, start in enumerate(me["starts"]):
            part = linear[i * rows : (i + 1) * rows]
            if first < 2 * cols:
                cosine = cos_ref[pl.ds(start, rows), :]
                sine = sin_ref[pl.ds(start, rows), :]
                heads = [part[:, h * HEAD_DIM : (h + 1) * HEAD_DIM] for h in range(2)]
                part = jnp.concatenate(
                    [x * cosine + pltpu.roll(x, HALF, 1) * sine for x in heads], axis=1
                )
            qkv[pl.ds(start, rows), first : first + step] = part.astype(jnp.bfloat16)
    attend(qkv, result, me["base"], total, rows, cols)
    copies = []
    for k in range(total):
        copy = pltpu.make_async_copy(result.at[k], outs[k], out_sems.at[k])
        copy.start()
        copies.append(copy)
    for copy in copies:
        copy.wait()


def attend(qkv, result, me, total, rows, cols):
    factor = HEAD_DIM ** (-0.5) * math.log2(math.e)
    below = lax.broadcasted_iota(jnp.int32, (rows, rows), 0) >= lax.broadcasted_iota(
        jnp.int32, (rows, rows), 1
    )

    def scored(q, k):
        return lax.dot_general(q, k, (((1,), (1,)), ((), ())), preferred_element_type=jnp.float32)

    for block in range(total):
        own, past = slice(block * rows, (block + 1) * rows), slice(0, block * rows)
        for head in range(cols // HEAD_DIM):
            lane = slice(head * HEAD_DIM, (head + 1) * HEAD_DIM)
            k_lane = slice(cols + lane.start, cols + lane.stop)
            v_lane = slice(2 * cols + lane.start, 2 * cols + lane.stop)
            q = qkv[own, lane]
            near = jnp.where(below, scored(q, qkv[own, k_lane]), -1e30)
            top = jnp.max(near, axis=1, keepdims=True)
            if block:
                far = scored(q, qkv[past, k_lane])
                top = jnp.maximum(top, jnp.max(far, axis=1, keepdims=True))
            top = top * factor
            expo = jnp.exp2(near * factor - top)
            bottom = jnp.sum(expo, axis=1, keepdims=True)
            numer = jnp.dot(expo.astype(jnp.bfloat16), qkv[own, v_lane], preferred_element_type=jnp.float32)
            if block:
                expo = jnp.exp2(far * factor - top)
                bottom += jnp.sum(expo, axis=1, keepdims=True)
                numer += jnp.dot(
                    expo.astype(jnp.bfloat16), qkv[past, v_lane], preferred_element_type=jnp.float32
                )
            result[block ^ me, :, lane] = (numer / bottom).astype(jnp.bfloat16)


def join_kernel(cols, total, own, *refs):
    pieces, out = refs[:total], refs[total]
    d, c = lax.axis_index("dp"), lax.axis_index("ctx")
    group = d % 2
    for k in range(total):
        base = c ^ k
        same = base // 2 == group
        plane = jnp.where(same, base, base ^ 2)
        core = jnp.where(same, group, 1 - group)
        lane = pl.ds(pl.multiple_of((2 * (plane % 2) + core) * cols, cols), cols)
        if k:
            out[0, :, lane] = pieces[k][...]
        else:
            out[0, :, lane] = jnp.where(c // 2 == group, own[...], pieces[k][...])


def fast(dp, ctx, tokens, norm_gain, q_weight, k_weight, v_weight):
    rows, features = tokens.shape[1], tokens.shape[2]
    cols = HEADS // ctx * HEAD_DIM
    every = [(d, c) for d in range(dp) for c in range(ctx)]

    def send(name, value, to):
        perm = [
            (d * ctx + c, to(d, c)[0] * ctx + to(d, c)[1]) for d, c in every if to(d, c) is not None
        ]
        with jax.named_scope(name):
            return lax.ppermute(value, ("dp", "ctx"), perm)

    def home(to):
        return lambda d, c: to(d, c) if c // 2 == d % 2 else None

    def away(to):
        return lambda d, c: to(d, c) if c // 2 != d % 2 else None

    d, c = lax.axis_index("dp"), lax.axis_index("ctx")

    def columns(heads):
        return jnp.concatenate(
            [lax.dynamic_slice_in_dim(w, heads * cols, cols, 1) for w in (q_weight, k_weight, v_weight)],
            axis=1,
        )

    own = tokens[0]
    heads = 2 * (c % 2) + d % 2
    core = lambda d, c: (d ^ 1, c)
    along_x = lambda d, c: (d ^ 2, c)
    along_y = lambda d, c: (d ^ 4, c)
    barrier = lambda *values: lax.optimization_barrier(values)
    kept, sent, w = {0: own}, {}, {}
    kept[1] = send("tokens_1", own, home(lambda d, c: (d, c ^ 1)))
    kept[2] = send("tokens_2", own, away(lambda d, c: (d, c ^ 2)))
    w[1] = send("weights_core", columns(heads ^ 1), core)
    w[0] = columns(heads)
    w[2] = send("weights_x", w[0], along_x)
    w[5] = send("weights_core_y", w[1], along_y)
    sent[0] = send("tokens_core_0", own, home(core))
    w[2], w[5], kept[1], sent[0] = barrier(w[2], w[5], kept[1], sent[0])
    w[6] = send("weights_xy", w[2], along_y)
    w[7] = send("weights_core_yx", w[5], along_x)
    sent[1] = send("tokens_core_1", kept[1], home(core))
    kept[2], w[2] = barrier(kept[2], w[2])
    kept[3] = send("tokens_3", kept[2], home(lambda d, c: (d, c ^ 1)))
    sent[2] = send("tokens_core_2", kept[2], home(core))
    sent[1], sent[2], w[0], w[1] = barrier(sent[1], sent[2], w[0], w[1])
    w[4] = send("weights_y", w[0], along_y)
    w[3] = send("weights_core_x", w[1], along_x)
    sent[3] = send("tokens_core_3", kept[3], home(core))
    kept, sent = [kept[i] for i in range(4)], [sent[i] for i in range(4)]
    cosine, sine = tables(ctx * rows)

    gain = norm_gain[None, :]
    any_space = pl.BlockSpec(memory_space=pl.ANY)
    vmem = pl.BlockSpec(memory_space=pltpu.VMEM)
    depth = q_weight.shape[0]
    partial, tail = pl.pallas_call(
        functools.partial(early_kernel, rows, cols),
        out_shape=[
            jax.ShapeDtypeStruct((ctx * rows, 3 * cols), jnp.float32),
            jax.ShapeDtypeStruct((ctx * rows, 2 * depth), jnp.bfloat16),
        ],
        in_specs=[any_space] * 14 + [vmem],
        out_specs=[vmem] * 2,
        scratch_shapes=[
            pltpu.VMEM((ctx * rows, features), jnp.bfloat16),
            pltpu.VMEM((ctx * rows, features), jnp.bfloat16),
            pltpu.VMEM((6 * depth, 3 * cols), jnp.bfloat16),
            pltpu.SemaphoreType.DMA((4,)),
            pltpu.SemaphoreType.DMA((6,)),
        ],
        compiler_params=pltpu.CompilerParams(vmem_limit_bytes=VMEM_LIMIT),
        cost_estimate=pl.CostEstimate(
            flops=2 * ctx * rows * 6 * depth * 3 * cols, bytes_accessed=10_000_000, transcendentals=0
        ),
        name="project_early",
    )(*kept, *sent, *[w[k] for k in (0, 1, 2, 5, 6, 7)], gain)
    pieces = pl.pallas_call(
        functools.partial(late_kernel, rows, cols, ctx),
        out_shape=[jax.ShapeDtypeStruct((rows, cols), jnp.bfloat16)] * ctx,
        in_specs=[any_space] * 2 + [vmem] * 4,
        out_specs=[any_space] * ctx,
        scratch_shapes=[
            pltpu.VMEM((2 * depth, 3 * cols), jnp.bfloat16),
            pltpu.VMEM((ctx * rows, 3 * cols), jnp.bfloat16),
            pltpu.VMEM((ctx, rows, cols), jnp.bfloat16),
            pltpu.SemaphoreType.DMA((2,)),
            pltpu.SemaphoreType.DMA((ctx,)),
        ],
        compiler_params=pltpu.CompilerParams(vmem_limit_bytes=VMEM_LIMIT),
        cost_estimate=pl.CostEstimate(
            flops=8_000_000_000, bytes_accessed=10_000_000, transcendentals=2_000_000
        ),
        name="attend",
    )(w[3], w[4], partial, tail, cosine, sine)

    def back(k):
        def to(d, c):
            base = c if c // 2 == d % 2 else c ^ 2
            target = ((d & 6) | (c // 2), base ^ k)
            return None if target == (d, c) else target

        return to

    arrived = [send(f"back_{k}", pieces[k], back(k)) for k in range(ctx)]
    return pl.pallas_call(
        functools.partial(join_kernel, cols, ctx),
        out_shape=jax.ShapeDtypeStruct((1, rows, ctx * cols), jnp.bfloat16),
        in_specs=[vmem] * (ctx + 1),
        out_specs=vmem,
        compiler_params=pltpu.CompilerParams(vmem_limit_bytes=8 * 1024 * 1024),
        name="join",
    )(pieces[0], *arrived)


def rotate(values, positions):
    heads = values.shape[1] // HEAD_DIM
    shaped = values.reshape(values.shape[0], heads, HEAD_DIM)
    freqs = 10000.0 ** (-(jnp.arange(HALF).astype(jnp.float32) * 2.0) / HEAD_DIM)
    angles = positions[:, None] * freqs[None, :]
    cosine = jnp.cos(angles)[:, None, :]
    sine = jnp.sin(angles)[:, None, :]
    first = shaped[:, :, :HALF]
    second = shaped[:, :, HALF:]
    return jnp.concatenate(
        [first * cosine - second * sine, second * cosine + first * sine], axis=2
    )


def general(dp, ctx, tokens, norm_gain, q_weight, k_weight, v_weight):
    rows = tokens.shape[1]
    heads = HEADS // ctx
    cols = heads * HEAD_DIM
    me = lax.axis_index("ctx")
    part = jnp.concatenate(
        [lax.dynamic_slice_in_dim(w, me * cols, cols, 1) for w in (q_weight, k_weight, v_weight)], axis=1
    )
    weights = lax.all_gather(part, "dp", axis=0, tiled=True)
    whole = lax.all_gather(tokens[0], "ctx", axis=0, tiled=True)
    normed = normalize(whole, norm_gain[None, :])
    linear = jnp.dot(normed, weights, preferred_element_type=jnp.float32)
    length = ctx * rows
    positions = jnp.arange(length).astype(jnp.float32)
    q = rotate(linear[:, :cols], positions).astype(jnp.bfloat16)
    k = rotate(linear[:, cols : 2 * cols], positions).astype(jnp.bfloat16)
    v = linear[:, 2 * cols :].astype(jnp.bfloat16).reshape(length, heads, HEAD_DIM)
    allowed = jnp.arange(length)[None, :] <= jnp.arange(length)[:, None]
    scores = jnp.einsum("qhd,khd->hqk", q, k, preferred_element_type=jnp.float32) * HEAD_DIM ** (-0.5)
    scores = jnp.where(allowed[None], scores, -1e30)
    top = jnp.max(scores, axis=2, keepdims=True)
    expo = jnp.where(allowed[None], jnp.exp(scores - top), 0.0)
    numer = jnp.einsum("hqk,khd->hqd", expo.astype(jnp.bfloat16), v, preferred_element_type=jnp.float32)
    result = (numer / jnp.sum(expo, axis=2, keepdims=True)).astype(jnp.bfloat16)
    result = result.reshape(heads, ctx, rows, HEAD_DIM).transpose(1, 2, 0, 3).reshape(ctx, rows, cols)
    back = lax.all_to_all(result, "ctx", 0, 0)
    return back.transpose(1, 0, 2).reshape(1, rows, ctx * cols)


def solution(mesh):
    dp, ctx = mesh.shape["dp"], mesh.shape["ctx"]
    body = fast if (dp, ctx) == (8, 4) else general
    placed = (P("dp", "ctx", None), P(), P("dp", None), P("dp", None), P("dp", None))
    return jax.shard_map(
        functools.partial(body, dp, ctx),
        mesh=mesh,
        in_specs=placed,
        out_specs=P("dp", "ctx", None),
        check_vma=False,
    )
```

```python
import functools
import math

import jax
import jax.numpy as jnp
from jax import lax
from jax.experimental import pallas as pl
from jax.experimental.pallas import tpu as pltpu
from jax.sharding import PartitionSpec as P

HEADS = 16
HEAD_DIM = 128
HALF = HEAD_DIM // 2
EPS = 1e-05
VMEM_LIMIT = 28 * 1024 * 1024

PLAN = {
    "order": ["t1", "t2", "w1", "w2", "w5", "u0", "w6", "w7", "u1", "t3", "u2", "w4", "w3", "u3"],
    "waits": [["w6", ["t1", "u0"]], ["w7", ["w2"]], ["t3", ["w2"]], ["w4", ["u1", "u2"]]],
    "early": [0, 1, 2, 5, 6, 7],
    "splits": [[0, 4]],
    "hold": [1, 2],
    "back": [0, 1, 2, 3],
    "direct3": False,
    "cross3": False,
    "cross5": False,
    "early_flops": 4000000000,
    "late_flops": 8000000000,
}


def tables(length):
    freqs = 10000.0 ** (-(jnp.arange(HALF).astype(jnp.float32) * 2.0) / HEAD_DIM)
    angles = jnp.arange(length).astype(jnp.float32)[:, None] * freqs[None, :]
    cosine = jnp.cos(angles)
    sine = jnp.sin(angles)
    return (
        jnp.concatenate([cosine, cosine], axis=1),
        jnp.concatenate([-sine, sine], axis=1),
    )


def normalize(block, gain):
    rows = block.astype(jnp.float32)
    scale = lax.rsqrt(jnp.mean(rows * rows, axis=1, keepdims=True) + EPS)
    return (rows * scale * gain.astype(jnp.float32)).astype(jnp.bfloat16)


def role(rows):
    d, c = lax.axis_index("dp"), lax.axis_index("ctx")
    home = c // 2 == d % 2
    return {
        "home": home,
        "starts": [pl.multiple_of((c ^ i) * rows, rows) for i in range(4)],
        "base": jnp.where(home, c, c ^ 2),
        "owner": d,
    }


def early_kernel(rows, order, early, groups, *refs):
    n = len(groups)
    kept, sent, shards = refs[:n], refs[n : 2 * n], refs[2 * n : 2 * n + early]
    gain, out, tail, held, normed, weights, token_sems, weight_sems = refs[2 * n + early :]
    me = role(rows)
    depth = shards[0].shape[0]
    loads = []
    row = 0
    for i in range(n):
        slot = held.at[pl.ds(row, kept[i].shape[0])]
        row += kept[i].shape[0]
        for condition, source in ((me["home"], kept[i]), (jnp.logical_not(me["home"]), sent[i])):

            @pl.when(condition)
            def _(source=source, slot=slot, i=i):
                pltpu.make_async_copy(source, slot, token_sems.at[i]).start()

        loads.append(pltpu.make_async_copy(kept[i], slot, token_sems.at[i]))
    weight_loads = []
    for i, shard in enumerate(shards):
        load = pltpu.make_async_copy(shard, weights.at[pl.ds(i * depth, depth)], weight_sems.at[i])
        load.start()
        weight_loads.append(load)
    lanes = []
    for owner in range(8):
        offset = me["owner"] ^ owner
        place = sum(jnp.where(offset == k, at, 0) for at, k in enumerate(order))
        lanes.append(pl.ds(pl.multiple_of(place * depth, depth), depth))
    at = 0
    for load, group in zip(loads, groups):
        load.wait()
        for _ in group:
            part = pl.ds(at * rows, rows)
            at += 1
            value = normalize(held[part, :], gain[...])
            for owner, lane in enumerate(lanes):
                normed[part, lane] = value[:, owner * depth : (owner + 1) * depth]
    for load in weight_loads:
        load.wait()
    first = early * depth
    tail[...] = normed[:, first:]
    step = 2 * HEAD_DIM
    for lane in range(0, out.shape[1], step):
        out[:, lane : lane + step] = jnp.dot(
            normed[:, :first], weights[:, lane : lane + step], preferred_element_type=jnp.float32
        )


def late_kernel(rows, cols, total, blocks, count, first_head, heads, *refs):
    shards = refs[:count]
    partial, tail, cos_ref, sin_ref = refs[count : count + 4]
    outs = refs[count + 4 : count + 4 + total]
    weights, qkv, result, weight_sems, out_sems = refs[count + 4 + total :]
    me = role(rows)
    depth = shards[0].shape[0]
    width = heads * HEAD_DIM
    start_lane = first_head * HEAD_DIM
    loads = []
    for i, shard in enumerate(shards):
        for j in range(3):
            load = pltpu.make_async_copy(
                shard.at[:, pl.ds(j * cols + start_lane, width)],
                weights.at[pl.ds(i * depth, depth), pl.ds(j * width, width)],
                weight_sems.at[3 * i + j],
            )
            load.start()
            loads.append(load)
    for load in loads:
        load.wait()
    step = HEAD_DIM if width % (2 * HEAD_DIM) else 2 * HEAD_DIM
    for j in range(3):
        for lane in range(0, width, step):
            first = j * cols + start_lane + lane
            linear = partial[:, first : first + step] + jnp.dot(
                tail[...],
                weights[:, j * width + lane : j * width + lane + step],
                preferred_element_type=jnp.float32,
            )
            for i, block in enumerate(blocks):
                start = me["starts"][block]
                value = linear[i * rows : (i + 1) * rows]
                if j < 2:
                    cosine = cos_ref[pl.ds(start, rows), :]
                    sine = sin_ref[pl.ds(start, rows), :]
                    parts = [value[:, h * HEAD_DIM : (h + 1) * HEAD_DIM] for h in range(step // HEAD_DIM)]
                    value = jnp.concatenate(
                        [x * cosine + pltpu.roll(x, HALF, 1) * sine for x in parts], axis=1
                    )
                lanes = slice(j * width + lane, j * width + lane + step)
                qkv[pl.ds(start, rows), lanes] = value.astype(jnp.bfloat16)
    attend(qkv, result, me["base"], total, rows, width)
    copies = []
    for k in range(total):
        copy = pltpu.make_async_copy(result.at[k], outs[k], out_sems.at[k])
        copy.start()
        copies.append(copy)
    for copy in copies:
        copy.wait()


def attend(qkv, result, me, total, rows, cols):
    factor = HEAD_DIM ** (-0.5) * math.log2(math.e)
    below = lax.broadcasted_iota(jnp.int32, (rows, rows), 0) >= lax.broadcasted_iota(
        jnp.int32, (rows, rows), 1
    )

    def scored(q, k):
        return lax.dot_general(q, k, (((1,), (1,)), ((), ())), preferred_element_type=jnp.float32)

    for block in range(total):
        own, past = slice(block * rows, (block + 1) * rows), slice(0, block * rows)
        for head in range(cols // HEAD_DIM):
            lane = slice(head * HEAD_DIM, (head + 1) * HEAD_DIM)
            k_lane = slice(cols + lane.start, cols + lane.stop)
            v_lane = slice(2 * cols + lane.start, 2 * cols + lane.stop)
            q = qkv[own, lane]
            near = jnp.where(below, scored(q, qkv[own, k_lane]), -1e30)
            top = jnp.max(near, axis=1, keepdims=True)
            if block:
                far = scored(q, qkv[past, k_lane])
                top = jnp.maximum(top, jnp.max(far, axis=1, keepdims=True))
            top = top * factor
            expo = jnp.exp2(near * factor - top)
            bottom = jnp.sum(expo, axis=1, keepdims=True)
            numer = jnp.dot(expo.astype(jnp.bfloat16), qkv[own, v_lane], preferred_element_type=jnp.float32)
            if block:
                expo = jnp.exp2(far * factor - top)
                bottom += jnp.sum(expo, axis=1, keepdims=True)
                numer += jnp.dot(
                    expo.astype(jnp.bfloat16), qkv[past, v_lane], preferred_element_type=jnp.float32
                )
            result[block ^ me, :, lane] = (numer / bottom).astype(jnp.bfloat16)


def join_kernel(cols, total, splits, *refs):
    out = refs[-1]
    d, c = lax.axis_index("dp"), lax.axis_index("ctx")
    group = d % 2
    for part, (first_head, heads) in enumerate(splits):
        own, *pieces = refs[part * (total + 1) : (part + 1) * (total + 1)]
        for k in range(total):
            base = c ^ k
            same = base // 2 == group
            plane = jnp.where(same, base, base ^ 2)
            core = jnp.where(same, group, 1 - group)
            first = (2 * (plane % 2) + core) * cols + first_head * HEAD_DIM
            lane = pl.ds(pl.multiple_of(first, HEAD_DIM), heads * HEAD_DIM)
            if k:
                out[0, :, lane] = pieces[k][...]
            else:
                out[0, :, lane] = jnp.where(c // 2 == group, own[...], pieces[k][...])


def fast(dp, ctx, tokens, norm_gain, q_weight, k_weight, v_weight):
    rows, features = tokens.shape[1], tokens.shape[2]
    cols = HEADS // ctx * HEAD_DIM
    depth = q_weight.shape[0]
    every = [(d, c) for d in range(dp) for c in range(ctx)]
    plan = PLAN

    def home(to):
        return lambda d, c: to(d, c) if c // 2 == d % 2 else None

    def away(to):
        return lambda d, c: to(d, c) if c // 2 != d % 2 else None

    shift = lambda k: lambda d, c: (d ^ k, c)
    plane = lambda k: lambda d, c: (d, c ^ k)
    routes = {
        "w1": ("o", shift(1)),
        "w2": ("m", shift(2)),
        "w4": ("m", shift(4)),
        "w6": ("w2", shift(4)),
        "w7": ("w5", shift(2)),
        "t1": ("own", home(plane(1))),
        "t2": ("own", away(plane(2))),
        "u0": ("own", home(shift(1))),
        "u1": ("t1", home(shift(1))),
        "u2": ("t2", home(shift(1))),
        "u3": ("t3", home(shift(1))),
    }
    routes["t3"] = ("own", away(plane(3))) if plan["direct3"] else ("t2", home(plane(1)))
    routes["w3"] = ("o", shift(3)) if plan["cross3"] else ("w1", shift(2))
    routes["w5"] = ("o", shift(5)) if plan["cross5"] else ("w1", shift(4))

    d, c = lax.axis_index("dp"), lax.axis_index("ctx")

    def columns(heads):
        return jnp.concatenate(
            [lax.dynamic_slice_in_dim(w, heads * cols, cols, 1) for w in (q_weight, k_weight, v_weight)],
            axis=1,
        )

    heads = 2 * (c % 2) + d % 2
    values = {"own": tokens[0], "o": columns(heads ^ 1), "m": columns(heads)}
    inputs = {}
    waits = {name: list(earlier) for name, earlier in plan["waits"]}

    for name in plan["order"]:
        source, to = routes[name]
        operand = values[source]
        earlier = waits.get(name, [])
        if earlier:
            operand, *late = lax.optimization_barrier((operand, *[values[e] for e in earlier]))
            values.update(zip(earlier, late))
        perm = [
            (dd * ctx + cc, to(dd, cc)[0] * ctx + to(dd, cc)[1])
            for dd, cc in every
            if to(dd, cc) is not None
        ]
        with jax.named_scope(name):
            values[name] = lax.ppermute(operand, ("dp", "ctx"), perm)
    cosine, sine = tables(ctx * rows)
    names = {0: "m", 1: "w1", 2: "w2", 3: "w3", 4: "w4", 5: "w5", 6: "w6", 7: "w7"}
    early = plan["early"]
    shard_order = early + [k for k in range(8) if k not in early]
    blocks = [0, 1, 2, 3]
    kept = [values[n] for n in ("own", "t1", "t2", "t3")]
    sent = [values[n] for n in ("u0", "u1", "u2", "u3")]

    gain = norm_gain[None, :]
    any_space = pl.BlockSpec(memory_space=pl.ANY)
    vmem = pl.BlockSpec(memory_space=pltpu.VMEM)
    n, late = len(early), 8 - len(early)
    partial, tail = pl.pallas_call(
        functools.partial(early_kernel, rows, shard_order, n, [[b] for b in blocks]),
        out_shape=[
            jax.ShapeDtypeStruct((ctx * rows, 3 * cols), jnp.float32),
            jax.ShapeDtypeStruct((ctx * rows, late * depth), jnp.bfloat16),
        ],
        in_specs=[any_space] * (8 + n) + [vmem],
        out_specs=[vmem] * 2,
        scratch_shapes=[
            pltpu.VMEM((ctx * rows, features), jnp.bfloat16),
            pltpu.VMEM((ctx * rows, features), jnp.bfloat16),
            pltpu.VMEM((n * depth, 3 * cols), jnp.bfloat16),
            pltpu.SemaphoreType.DMA((4,)),
            pltpu.SemaphoreType.DMA((n,)),
        ],
        compiler_params=pltpu.CompilerParams(vmem_limit_bytes=VMEM_LIMIT),
        cost_estimate=pl.CostEstimate(
            flops=plan["early_flops"], bytes_accessed=1_000_000, transcendentals=0
        ),
        name="project_early",
    )(*kept, *sent, *[values[names[k]] for k in early], gain)

    def back(k):
        def to(d, c):
            base = c if c // 2 == d % 2 else c ^ 2
            target = ((d & 6) | (c // 2), base ^ k)
            return None if target == (d, c) else target

        return to

    arrived = []
    last = [values[names[k]] for k in shard_order[n:]]
    for part, (first_head, count) in enumerate(plan["splits"]):
        width = count * HEAD_DIM
        pieces = pl.pallas_call(
            functools.partial(late_kernel, rows, cols, ctx, blocks, late, first_head, count),
            out_shape=[jax.ShapeDtypeStruct((rows, width), jnp.bfloat16)] * ctx,
            in_specs=[any_space] * late + [vmem] * 4,
            out_specs=[any_space] * ctx,
            scratch_shapes=[
                pltpu.VMEM((late * depth, 3 * width), jnp.bfloat16),
                pltpu.VMEM((ctx * rows, 3 * width), jnp.bfloat16),
                pltpu.VMEM((ctx, rows, width), jnp.bfloat16),
                pltpu.SemaphoreType.DMA((3 * late,)),
                pltpu.SemaphoreType.DMA((ctx,)),
            ],
            compiler_params=pltpu.CompilerParams(vmem_limit_bytes=VMEM_LIMIT),
            cost_estimate=pl.CostEstimate(
                flops=plan["late_flops"], bytes_accessed=1_000_000, transcendentals=0
            ),
            name=f"attend_{part}",
        )(*last, partial, tail, cosine, sine)
        if arrived:
            hold = plan["hold"]
            both = lax.optimization_barrier((*[arrived[-ctx + k] for k in hold], *pieces))
            for k, value in zip(hold, both):
                arrived[-ctx + k] = value
            pieces = both[len(hold) :]
        elif len(plan["splits"]) > 1:
            pieces = list(pieces)
            pieces[0], last[0] = lax.optimization_barrier((pieces[0], last[0]))
        moved = {}
        for k in plan["back"]:
            with jax.named_scope(f"back_{part}_{k}"):
                to = back(k)
                perm = [
                    (dd * ctx + cc, to(dd, cc)[0] * ctx + to(dd, cc)[1])
                    for dd, cc in every
                    if to(dd, cc) is not None
                ]
                moved[k] = lax.ppermute(pieces[k], ("dp", "ctx"), perm)
        arrived += [pieces[0]] + [moved[k] for k in range(ctx)]
    return pl.pallas_call(
        functools.partial(join_kernel, cols, ctx, plan["splits"]),
        out_shape=jax.ShapeDtypeStruct((1, rows, ctx * cols), jnp.bfloat16),
        in_specs=[vmem] * len(arrived),
        out_specs=vmem,
        compiler_params=pltpu.CompilerParams(vmem_limit_bytes=8 * 1024 * 1024),
        name="join",
    )(*arrived)


def rotate(values, positions):
    heads = values.shape[1] // HEAD_DIM
    shaped = values.reshape(values.shape[0], heads, HEAD_DIM)
    freqs = 10000.0 ** (-(jnp.arange(HALF).astype(jnp.float32) * 2.0) / HEAD_DIM)
    angles = positions[:, None] * freqs[None, :]
    cosine = jnp.cos(angles)[:, None, :]
    sine = jnp.sin(angles)[:, None, :]
    first = shaped[:, :, :HALF]
    second = shaped[:, :, HALF:]
    return jnp.concatenate(
        [first * cosine - second * sine, second * cosine + first * sine], axis=2
    )


def general(dp, ctx, tokens, norm_gain, q_weight, k_weight, v_weight):
    rows = tokens.shape[1]
    heads = HEADS // ctx
    cols = heads * HEAD_DIM
    me = lax.axis_index("ctx")
    part = jnp.concatenate(
        [lax.dynamic_slice_in_dim(w, me * cols, cols, 1) for w in (q_weight, k_weight, v_weight)], axis=1
    )
    weights = lax.all_gather(part, "dp", axis=0, tiled=True)
    whole = lax.all_gather(tokens[0], "ctx", axis=0, tiled=True)
    normed = normalize(whole, norm_gain[None, :])
    linear = jnp.dot(normed, weights, preferred_element_type=jnp.float32)
    length = ctx * rows
    positions = jnp.arange(length).astype(jnp.float32)
    q = rotate(linear[:, :cols], positions).astype(jnp.bfloat16)
    k = rotate(linear[:, cols : 2 * cols], positions).astype(jnp.bfloat16)
    v = linear[:, 2 * cols :].astype(jnp.bfloat16).reshape(length, heads, HEAD_DIM)
    allowed = jnp.arange(length)[None, :] <= jnp.arange(length)[:, None]
    scores = jnp.einsum("qhd,khd->hqk", q, k, preferred_element_type=jnp.float32) * HEAD_DIM ** (-0.5)
    scores = jnp.where(allowed[None], scores, -1e30)
    top = jnp.max(scores, axis=2, keepdims=True)
    expo = jnp.where(allowed[None], jnp.exp(scores - top), 0.0)
    numer = jnp.einsum("hqk,khd->hqd", expo.astype(jnp.bfloat16), v, preferred_element_type=jnp.float32)
    result = (numer / jnp.sum(expo, axis=2, keepdims=True)).astype(jnp.bfloat16)
    result = result.reshape(heads, ctx, rows, HEAD_DIM).transpose(1, 2, 0, 3).reshape(ctx, rows, cols)
    back = lax.all_to_all(result, "ctx", 0, 0)
    return back.transpose(1, 0, 2).reshape(1, rows, ctx * cols)


def solution(mesh):
    dp, ctx = mesh.shape["dp"], mesh.shape["ctx"]
    body = fast if (dp, ctx) == (8, 4) else general
    placed = (P("dp", "ctx", None), P(), P("dp", None), P("dp", None), P("dp", None))
    return jax.shard_map(
        functools.partial(body, dp, ctx),
        mesh=mesh,
        in_specs=placed,
        out_specs=P("dp", "ctx", None),
        check_vma=False,
    )
```

```python
import functools
import math

import jax
import jax.numpy as jnp
from jax import lax
from jax.experimental import pallas as pl
from jax.experimental.pallas import tpu as pltpu
from jax.sharding import PartitionSpec as P

HEADS = 16
HEAD_DIM = 128
HALF = HEAD_DIM // 2
EPS = 1e-05
VMEM_LIMIT = 28 * 1024 * 1024

PLAN = {
    "order": ["t2", "w1", "u0", "w2", "w5", "w7", "t3", "u2", "w3", "u3", "t1", "w6", "u1", "w4"],
    "waits": [["w6", ["t1", "u0"]], ["w7", ["w2"]], ["t3", ["w2"]], ["w4", ["u1", "u2"]], ["t1", ["cos", "sin"]]],
    "early": [0, 1, 2, 5, 6, 7],
    "splits": [[0, 4]],
    "hold": [0, 1, 2, 3],
    "back": [1, 0, 3, 2],
    "direct3": False,
    "cross3": False,
    "cross5": False,
    "early_flops": 4000000000,
    "late_flops": 1000000,
    "norm_flops": 4000000000,
    "join": [1, 0, 3, 2],
}


def tables(length):
    freqs = 10000.0 ** (-(jnp.arange(HALF).astype(jnp.float32) * 2.0) / HEAD_DIM)
    angles = jnp.arange(length).astype(jnp.float32)[:, None] * freqs[None, :]
    cosine = jnp.cos(angles)
    sine = jnp.sin(angles)
    return (
        jnp.concatenate([cosine, cosine], axis=1),
        jnp.concatenate([-sine, sine], axis=1),
    )


def normalize(block, gain):
    rows = block.astype(jnp.float32)
    scale = lax.rsqrt(jnp.mean(rows * rows, axis=1, keepdims=True) + EPS)
    return (rows * scale * gain.astype(jnp.float32)).astype(jnp.bfloat16)


def role(rows):
    d, c = lax.axis_index("dp"), lax.axis_index("ctx")
    home = c // 2 == d % 2
    return {
        "home": home,
        "starts": [pl.multiple_of((c ^ i) * rows, rows) for i in range(4)],
        "base": jnp.where(home, c, c ^ 2),
        "owner": d,
    }


def norm_kernel(rows, order, *refs):
    kept, sent, shards = refs[:4], refs[4:8], refs[8:12]
    gain, out, weights, held, token_sems, weight_sems = refs[12:]
    me = role(rows)
    depth = shards[0].shape[0]
    loads = []
    for i in range(4):
        slot = held.at[pl.ds(i * rows, rows)]
        for condition, source in ((me["home"], kept[i]), (jnp.logical_not(me["home"]), sent[i])):

            @pl.when(condition)
            def _(source=source, slot=slot, i=i):
                pltpu.make_async_copy(source, slot, token_sems.at[i]).start()

        loads.append(pltpu.make_async_copy(kept[i], slot, token_sems.at[i]))
    weight_loads = []
    for i, shard in enumerate(shards):
        load = pltpu.make_async_copy(shard, weights.at[pl.ds(i * depth, depth)], weight_sems.at[i])
        load.start()
        weight_loads.append(load)
    lanes = []
    for owner in range(8):
        offset = me["owner"] ^ owner
        place = sum(jnp.where(offset == k, at, 0) for at, k in enumerate(order))
        lanes.append(pl.ds(pl.multiple_of(place * depth, depth), depth))
    for i in range(4):
        loads[i].wait()
        part = pl.ds(i * rows, rows)
        value = normalize(held[part, :], gain[...])
        for owner, lane in enumerate(lanes):
            out[part, lane] = value[:, owner * depth : (owner + 1) * depth]
    for load in weight_loads:
        load.wait()


def load_shards(shards, weights, sems, lanes):
    depth = shards[0].shape[0]
    loads = []
    for i, shard in enumerate(shards):
        for j, (source, target, width) in enumerate(lanes):
            load = pltpu.make_async_copy(
                shard.at[:, pl.ds(source, width)],
                weights.at[pl.ds(i * depth, depth), pl.ds(target, width)],
                sems.at[len(lanes) * i + j],
            )
            load.start()
            loads.append(load)
    return loads


def early_kernel(*refs):
    normed, first, shards, out, weights, sems = refs[0], refs[1], refs[2:-3], *refs[-3:]
    columns = out.shape[1]
    loads = load_shards(shards, weights, sems, [(0, 0, columns)])
    for load in loads:
        load.wait()
    middle, end = first.shape[0], first.shape[0] + weights.shape[0]
    step = 2 * HEAD_DIM
    for lane in range(0, columns, step):
        lanes = slice(lane, lane + step)
        out[:, lanes] = jnp.dot(
            normed[:, :middle], first[:, lanes], preferred_element_type=jnp.float32
        ) + jnp.dot(normed[:, middle:end], weights[:, lanes], preferred_element_type=jnp.float32)


def late_kernel(rows, cols, total, count, first_head, heads, *refs):
    shards = refs[:count]
    partial, normed, cos_ref, sin_ref = refs[count : count + 4]
    outs = refs[count + 4 : count + 4 + total]
    weights, qkv, result, weight_sems, out_sems = refs[count + 4 + total :]
    me = role(rows)
    width = heads * HEAD_DIM
    start_lane = first_head * HEAD_DIM
    loads = load_shards(
        shards, weights, weight_sems, [(j * cols + start_lane, j * width, width) for j in range(3)]
    )
    for load in loads:
        load.wait()
    tail = normed.shape[1] - weights.shape[0]
    step = HEAD_DIM if width % (2 * HEAD_DIM) else 2 * HEAD_DIM
    for j in range(3):
        for lane in range(0, width, step):
            first = j * cols + start_lane + lane
            linear = partial[:, first : first + step] + jnp.dot(
                normed[:, tail:],
                weights[:, j * width + lane : j * width + lane + step],
                preferred_element_type=jnp.float32,
            )
            for i, start in enumerate(me["starts"]):
                value = linear[i * rows : (i + 1) * rows]
                if j < 2:
                    cosine = cos_ref[pl.ds(start, rows), :]
                    sine = sin_ref[pl.ds(start, rows), :]
                    parts = [value[:, h * HEAD_DIM : (h + 1) * HEAD_DIM] for h in range(step // HEAD_DIM)]
                    value = jnp.concatenate(
                        [x * cosine + pltpu.roll(x, HALF, 1) * sine for x in parts], axis=1
                    )
                lanes = slice(j * width + lane, j * width + lane + step)
                qkv[pl.ds(start, rows), lanes] = value.astype(jnp.bfloat16)
    attend(qkv, result, me["base"], total, rows, width)
    copies = []
    for k in range(total):
        copy = pltpu.make_async_copy(result.at[k], outs[k], out_sems.at[k])
        copy.start()
        copies.append(copy)
    for copy in copies:
        copy.wait()


def attend(qkv, result, me, total, rows, cols):
    factor = HEAD_DIM ** (-0.5) * math.log2(math.e)
    below = lax.broadcasted_iota(jnp.int32, (rows, rows), 0) >= lax.broadcasted_iota(
        jnp.int32, (rows, rows), 1
    )

    def scored(q, k):
        return lax.dot_general(q, k, (((1,), (1,)), ((), ())), preferred_element_type=jnp.float32)

    for block in range(total):
        own, past = slice(block * rows, (block + 1) * rows), slice(0, block * rows)
        for head in range(cols // HEAD_DIM):
            lane = slice(head * HEAD_DIM, (head + 1) * HEAD_DIM)
            k_lane = slice(cols + lane.start, cols + lane.stop)
            v_lane = slice(2 * cols + lane.start, 2 * cols + lane.stop)
            q = qkv[own, lane]
            near = jnp.where(below, scored(q, qkv[own, k_lane]), -1e30)
            top = jnp.max(near, axis=1, keepdims=True)
            if block:
                far = scored(q, qkv[past, k_lane])
                top = jnp.maximum(top, jnp.max(far, axis=1, keepdims=True))
            top = top * factor
            expo = jnp.exp2(near * factor - top)
            bottom = jnp.sum(expo, axis=1, keepdims=True)
            numer = jnp.dot(expo.astype(jnp.bfloat16), qkv[own, v_lane], preferred_element_type=jnp.float32)
            if block:
                expo = jnp.exp2(far * factor - top)
                bottom += jnp.sum(expo, axis=1, keepdims=True)
                numer += jnp.dot(
                    expo.astype(jnp.bfloat16), qkv[past, v_lane], preferred_element_type=jnp.float32
                )
            result[block ^ me, :, lane] = (numer / bottom).astype(jnp.bfloat16)


def join_kernel(cols, total, splits, order, *refs):
    out = refs[-1]
    d, c = lax.axis_index("dp"), lax.axis_index("ctx")
    group = d % 2
    for part, (first_head, heads) in enumerate(splits):
        own, *pieces = refs[part * (total + 1) : (part + 1) * (total + 1)]
        for piece, k in zip(pieces, order):
            base = c ^ k
            same = base // 2 == group
            plane = jnp.where(same, base, base ^ 2)
            core = jnp.where(same, group, 1 - group)
            first = (2 * (plane % 2) + core) * cols + first_head * HEAD_DIM
            lane = pl.ds(pl.multiple_of(first, HEAD_DIM), heads * HEAD_DIM)
            if k:
                out[0, :, lane] = piece[...]
            else:
                out[0, :, lane] = jnp.where(c // 2 == group, own[...], piece[...])


def fast(dp, ctx, tokens, norm_gain, q_weight, k_weight, v_weight):
    rows, features = tokens.shape[1], tokens.shape[2]
    cols = HEADS // ctx * HEAD_DIM
    depth = q_weight.shape[0]
    every = [(d, c) for d in range(dp) for c in range(ctx)]
    plan = PLAN

    def home(to):
        return lambda d, c: to(d, c) if c // 2 == d % 2 else None

    def away(to):
        return lambda d, c: to(d, c) if c // 2 != d % 2 else None

    shift = lambda k: lambda d, c: (d ^ k, c)
    plane = lambda k: lambda d, c: (d, c ^ k)
    routes = {
        "w1": ("o", shift(1)),
        "w2": ("m", shift(2)),
        "w4": ("m", shift(4)),
        "w6": ("w2", shift(4)),
        "w7": ("w5", shift(2)),
        "t1": ("own", home(plane(1))),
        "t2": ("own", away(plane(2))),
        "u0": ("own", home(shift(1))),
        "u1": ("t1", home(shift(1))),
        "u2": ("t2", home(shift(1))),
        "u3": ("t3", home(shift(1))),
    }
    routes["t3"] = ("own", away(plane(3))) if plan["direct3"] else ("t2", home(plane(1)))
    routes["w3"] = ("o", shift(3)) if plan["cross3"] else ("w1", shift(2))
    routes["w5"] = ("o", shift(5)) if plan["cross5"] else ("w1", shift(4))

    d, c = lax.axis_index("dp"), lax.axis_index("ctx")

    def columns(heads):
        return jnp.concatenate(
            [lax.dynamic_slice_in_dim(w, heads * cols, cols, 1) for w in (q_weight, k_weight, v_weight)],
            axis=1,
        )

    heads = 2 * (c % 2) + d % 2
    values = {"own": tokens[0], "o": columns(heads ^ 1), "m": columns(heads)}
    values["cos"], values["sin"] = tables(ctx * rows)
    waits = {name: list(earlier) for name, earlier in plan["waits"]}

    for name in plan["order"]:
        source, to = routes[name]
        operand = values[source]
        earlier = waits.get(name, [])
        if earlier:
            operand, *late = lax.optimization_barrier((operand, *[values[e] for e in earlier]))
            values.update(zip(earlier, late))
        perm = [
            (dd * ctx + cc, to(dd, cc)[0] * ctx + to(dd, cc)[1])
            for dd, cc in every
            if to(dd, cc) is not None
        ]
        with jax.named_scope(name):
            values[name] = lax.ppermute(operand, ("dp", "ctx"), perm)
    cosine, sine = values["cos"], values["sin"]
    names = {0: "m", 1: "w1", 2: "w2", 3: "w3", 4: "w4", 5: "w5", 6: "w6", 7: "w7"}
    early = plan["early"]
    shard_order = early + [k for k in range(8) if k not in early]
    kept = [values[n] for n in ("own", "t1", "t2", "t3")]
    sent = [values[n] for n in ("u0", "u1", "u2", "u3")]

    gain = norm_gain[None, :]
    any_space = pl.BlockSpec(memory_space=pl.ANY)
    vmem = pl.BlockSpec(memory_space=pltpu.VMEM)
    n, late = len(early), 8 - len(early)
    length = ctx * rows
    normed, first = pl.pallas_call(
        functools.partial(norm_kernel, rows, shard_order),
        out_shape=[
            jax.ShapeDtypeStruct((length, features), jnp.bfloat16),
            jax.ShapeDtypeStruct((4 * depth, 3 * cols), jnp.bfloat16),
        ],
        in_specs=[any_space] * 12 + [vmem],
        out_specs=[vmem] * 2,
        scratch_shapes=[
            pltpu.VMEM((length, features), jnp.bfloat16),
            pltpu.SemaphoreType.DMA((4,)),
            pltpu.SemaphoreType.DMA((4,)),
        ],
        compiler_params=pltpu.CompilerParams(vmem_limit_bytes=VMEM_LIMIT),
        cost_estimate=pl.CostEstimate(
            flops=plan["norm_flops"], bytes_accessed=1_000_000, transcendentals=0
        ),
        name="normalize",
    )(*kept, *sent, *[values[names[k]] for k in early[:4]], gain)
    partial = pl.pallas_call(
        early_kernel,
        out_shape=jax.ShapeDtypeStruct((length, 3 * cols), jnp.float32),
        in_specs=[vmem] * 2 + [any_space] * (n - 4),
        out_specs=vmem,
        scratch_shapes=[
            pltpu.VMEM(((n - 4) * depth, 3 * cols), jnp.bfloat16),
            pltpu.SemaphoreType.DMA((n - 4,)),
        ],
        compiler_params=pltpu.CompilerParams(vmem_limit_bytes=VMEM_LIMIT),
        cost_estimate=pl.CostEstimate(
            flops=plan["early_flops"], bytes_accessed=1_000_000, transcendentals=0
        ),
        name="project_early",
    )(normed, first, *[values[names[k]] for k in early[4:]])

    def back(k):
        def to(d, c):
            base = c if c // 2 == d % 2 else c ^ 2
            target = ((d & 6) | (c // 2), base ^ k)
            return None if target == (d, c) else target

        return to

    arrived = []
    last = [values[names[k]] for k in shard_order[n:]]
    for part, (first_head, count) in enumerate(plan["splits"]):
        width = count * HEAD_DIM
        pieces = pl.pallas_call(
            functools.partial(late_kernel, rows, cols, ctx, late, first_head, count),
            out_shape=[jax.ShapeDtypeStruct((rows, width), jnp.bfloat16)] * ctx,
            in_specs=[any_space] * late + [vmem] * 4,
            out_specs=[any_space] * ctx,
            scratch_shapes=[
                pltpu.VMEM((late * depth, 3 * width), jnp.bfloat16),
                pltpu.VMEM((ctx * rows, 3 * width), jnp.bfloat16),
                pltpu.VMEM((ctx, rows, width), jnp.bfloat16),
                pltpu.SemaphoreType.DMA((3 * late,)),
                pltpu.SemaphoreType.DMA((ctx,)),
            ],
            compiler_params=pltpu.CompilerParams(vmem_limit_bytes=VMEM_LIMIT),
            cost_estimate=pl.CostEstimate(
                flops=plan["late_flops"], bytes_accessed=1_000_000, transcendentals=0
            ),
            name=f"attend_{part}",
        )(*last, partial, normed, cosine, sine)
        if arrived:
            hold = plan["hold"]
            both = lax.optimization_barrier((*[arrived[-ctx + k] for k in hold], *pieces))
            for k, value in zip(hold, both):
                arrived[-ctx + k] = value
            pieces = both[len(hold) :]
        elif len(plan["splits"]) > 1:
            pieces = list(pieces)
            pieces[0], last[0] = lax.optimization_barrier((pieces[0], last[0]))
        moved = {}
        for k in plan["back"]:
            with jax.named_scope(f"back_{part}_{k}"):
                to = back(k)
                perm = [
                    (dd * ctx + cc, to(dd, cc)[0] * ctx + to(dd, cc)[1])
                    for dd, cc in every
                    if to(dd, cc) is not None
                ]
                moved[k] = lax.ppermute(pieces[k], ("dp", "ctx"), perm)
        arrived += [pieces[0]] + [moved[k] for k in plan["join"]]
    return pl.pallas_call(
        functools.partial(join_kernel, cols, ctx, plan["splits"], plan["join"]),
        out_shape=jax.ShapeDtypeStruct((1, rows, ctx * cols), jnp.bfloat16),
        in_specs=[vmem] * len(arrived),
        out_specs=vmem,
        compiler_params=pltpu.CompilerParams(vmem_limit_bytes=8 * 1024 * 1024),
        name="join",
    )(*arrived)


def rotate(values, positions):
    heads = values.shape[1] // HEAD_DIM
    shaped = values.reshape(values.shape[0], heads, HEAD_DIM)
    freqs = 10000.0 ** (-(jnp.arange(HALF).astype(jnp.float32) * 2.0) / HEAD_DIM)
    angles = positions[:, None] * freqs[None, :]
    cosine = jnp.cos(angles)[:, None, :]
    sine = jnp.sin(angles)[:, None, :]
    first = shaped[:, :, :HALF]
    second = shaped[:, :, HALF:]
    return jnp.concatenate(
        [first * cosine - second * sine, second * cosine + first * sine], axis=2
    )


def general(dp, ctx, tokens, norm_gain, q_weight, k_weight, v_weight):
    rows = tokens.shape[1]
    heads = HEADS // ctx
    cols = heads * HEAD_DIM
    me = lax.axis_index("ctx")
    part = jnp.concatenate(
        [lax.dynamic_slice_in_dim(w, me * cols, cols, 1) for w in (q_weight, k_weight, v_weight)], axis=1
    )
    weights = lax.all_gather(part, "dp", axis=0, tiled=True)
    whole = lax.all_gather(tokens[0], "ctx", axis=0, tiled=True)
    normed = normalize(whole, norm_gain[None, :])
    linear = jnp.dot(normed, weights, preferred_element_type=jnp.float32)
    length = ctx * rows
    positions = jnp.arange(length).astype(jnp.float32)
    q = rotate(linear[:, :cols], positions).astype(jnp.bfloat16)
    k = rotate(linear[:, cols : 2 * cols], positions).astype(jnp.bfloat16)
    v = linear[:, 2 * cols :].astype(jnp.bfloat16).reshape(length, heads, HEAD_DIM)
    allowed = jnp.arange(length)[None, :] <= jnp.arange(length)[:, None]
    scores = jnp.einsum("qhd,khd->hqk", q, k, preferred_element_type=jnp.float32) * HEAD_DIM ** (-0.5)
    scores = jnp.where(allowed[None], scores, -1e30)
    top = jnp.max(scores, axis=2, keepdims=True)
    expo = jnp.where(allowed[None], jnp.exp(scores - top), 0.0)
    numer = jnp.einsum("hqk,khd->hqd", expo.astype(jnp.bfloat16), v, preferred_element_type=jnp.float32)
    result = (numer / jnp.sum(expo, axis=2, keepdims=True)).astype(jnp.bfloat16)
    result = result.reshape(heads, ctx, rows, HEAD_DIM).transpose(1, 2, 0, 3).reshape(ctx, rows, cols)
    back = lax.all_to_all(result, "ctx", 0, 0)
    return back.transpose(1, 0, 2).reshape(1, rows, ctx * cols)


def solution(mesh):
    dp, ctx = mesh.shape["dp"], mesh.shape["ctx"]
    body = fast if (dp, ctx) == (8, 4) else general
    placed = (P("dp", "ctx", None), P(), P("dp", None), P("dp", None), P("dp", None))
    return jax.shard_map(
        functools.partial(body, dp, ctx),
        mesh=mesh,
        in_specs=placed,
        out_specs=P("dp", "ctx", None),
        check_vma=False,
    )
```

```python
import functools
import math

import jax
import jax.numpy as jnp
from jax import lax
from jax.experimental import pallas as pl
from jax.experimental.pallas import tpu as pltpu
from jax.sharding import PartitionSpec as P

HEADS = 16
HEAD_DIM = 128
HALF = HEAD_DIM // 2
EPS = 1e-05
VMEM_LIMIT = 28 * 1024 * 1024

PLAN = {
    "order": ["t2", "w1", "u0", "w2", "w5", "w7", "t3", "u2", "w3", "u3", "t1", "w6", "u1", "w4"],
    "waits": [["w6", ["t1", "u0"]], ["w7", ["w2"]], ["t3", ["w2"]], ["w4", ["u1", "u2"]], ["t1", ["cos", "sin"]]],
    "early": [0, 1, 2, 5, 6, 7],
    "splits": [[0, 4]],
    "hold": [],
    "back": [1, 0, 3, 2],
    "direct3": False,
    "cross3": False,
    "cross5": False,
    "early_flops": 4000000000,
    "late_flops": 1000000,
    "norm_flops": 4000000000,
    "join": [1, 0, 3, 2],
}


def tables(length):
    freqs = 10000.0 ** (-(jnp.arange(HALF).astype(jnp.float32) * 2.0) / HEAD_DIM)
    angles = jnp.arange(length).astype(jnp.float32)[:, None] * freqs[None, :]
    cosine = jnp.cos(angles)
    sine = jnp.sin(angles)
    return (
        jnp.concatenate([cosine, cosine], axis=1),
        jnp.concatenate([-sine, sine], axis=1),
    )


def normalize(block, gain):
    rows = block.astype(jnp.float32)
    scale = lax.rsqrt(jnp.mean(rows * rows, axis=1, keepdims=True) + EPS)
    return (rows * scale * gain.astype(jnp.float32)).astype(jnp.bfloat16)


def role(rows):
    d, c = lax.axis_index("dp"), lax.axis_index("ctx")
    home = c // 2 == d % 2
    return {
        "home": home,
        "starts": [pl.multiple_of((c ^ i) * rows, rows) for i in range(4)],
        "base": jnp.where(home, c, c ^ 2),
        "owner": d,
    }


def norm_kernel(rows, order, *refs):
    kept, sent, shards = refs[:4], refs[4:8], refs[8:12]
    gain, out, weights, held, token_sems, weight_sems = refs[12:]
    me = role(rows)
    depth = shards[0].shape[0]
    loads = []
    for i in range(4):
        slot = held.at[pl.ds(i * rows, rows)]
        for condition, source in ((me["home"], kept[i]), (jnp.logical_not(me["home"]), sent[i])):

            @pl.when(condition)
            def _(source=source, slot=slot, i=i):
                pltpu.make_async_copy(source, slot, token_sems.at[i]).start()

        loads.append(pltpu.make_async_copy(kept[i], slot, token_sems.at[i]))
    weight_loads = []
    for i, shard in enumerate(shards):
        load = pltpu.make_async_copy(shard, weights.at[pl.ds(i * depth, depth)], weight_sems.at[i])
        load.start()
        weight_loads.append(load)
    lanes = []
    for owner in range(8):
        offset = me["owner"] ^ owner
        place = sum(jnp.where(offset == k, at, 0) for at, k in enumerate(order))
        lanes.append(pl.ds(pl.multiple_of(place * depth, depth), depth))
    for i in range(4):
        loads[i].wait()
        part = pl.ds(i * rows, rows)
        value = normalize(held[part, :], gain[...])
        for owner, lane in enumerate(lanes):
            out[part, lane] = value[:, owner * depth : (owner + 1) * depth]
    for load in weight_loads:
        load.wait()


def load_shards(shards, weights, sems, lanes):
    depth = shards[0].shape[0]
    loads = []
    for i, shard in enumerate(shards):
        for j, (source, target, width) in enumerate(lanes):
            load = pltpu.make_async_copy(
                shard.at[:, pl.ds(source, width)],
                weights.at[pl.ds(i * depth, depth), pl.ds(target, width)],
                sems.at[len(lanes) * i + j],
            )
            load.start()
            loads.append(load)
    return loads


def early_kernel(*refs):
    normed, first, shards, out, weights, sems = refs[0], refs[1], refs[2:-3], *refs[-3:]
    columns = out.shape[1]
    loads = load_shards(shards, weights, sems, [(0, 0, columns)])
    for load in loads:
        load.wait()
    middle, end = first.shape[0], first.shape[0] + weights.shape[0]
    step = 2 * HEAD_DIM
    for lane in range(0, columns, step):
        lanes = slice(lane, lane + step)
        out[:, lanes] = jnp.dot(
            normed[:, :middle], first[:, lanes], preferred_element_type=jnp.float32
        ) + jnp.dot(normed[:, middle:end], weights[:, lanes], preferred_element_type=jnp.float32)


def late_kernel(rows, cols, total, count, first_head, heads, *refs):
    shards = refs[:count]
    partial, normed, cos_ref, sin_ref = refs[count : count + 4]
    outs = refs[count + 4 : count + 4 + total]
    weights, qkv, result, weight_sems, out_sems = refs[count + 4 + total :]
    me = role(rows)
    width = heads * HEAD_DIM
    start_lane = first_head * HEAD_DIM
    loads = load_shards(
        shards, weights, weight_sems, [(j * cols + start_lane, j * width, width) for j in range(3)]
    )
    tail = normed.shape[1] - weights.shape[0]
    step = HEAD_DIM if width % (2 * HEAD_DIM) else 2 * HEAD_DIM
    for j in range(3):
        for load in loads[j::3]:
            load.wait()
        for lane in range(0, width, step):
            first = j * cols + start_lane + lane
            linear = partial[:, first : first + step] + jnp.dot(
                normed[:, tail:],
                weights[:, j * width + lane : j * width + lane + step],
                preferred_element_type=jnp.float32,
            )
            for i, start in enumerate(me["starts"]):
                value = linear[i * rows : (i + 1) * rows]
                if j < 2:
                    cosine = cos_ref[pl.ds(start, rows), :]
                    sine = sin_ref[pl.ds(start, rows), :]
                    parts = [value[:, h * HEAD_DIM : (h + 1) * HEAD_DIM] for h in range(step // HEAD_DIM)]
                    value = jnp.concatenate(
                        [x * cosine + pltpu.roll(x, HALF, 1) * sine for x in parts], axis=1
                    )
                lanes = slice(j * width + lane, j * width + lane + step)
                qkv[pl.ds(start, rows), lanes] = value.astype(jnp.bfloat16)
    attend(qkv, result, me["base"], total, rows, width)
    copies = []
    for k in range(total):
        copy = pltpu.make_async_copy(result.at[k], outs[k], out_sems.at[k])
        copy.start()
        copies.append(copy)
    for copy in copies:
        copy.wait()


def attend(qkv, result, me, total, rows, cols):
    factor = HEAD_DIM ** (-0.5) * math.log2(math.e)
    below = lax.broadcasted_iota(jnp.int32, (rows, rows), 0) >= lax.broadcasted_iota(
        jnp.int32, (rows, rows), 1
    )

    def scored(q, k):
        return lax.dot_general(q, k, (((1,), (1,)), ((), ())), preferred_element_type=jnp.float32)

    for block in range(total):
        own, past = slice(block * rows, (block + 1) * rows), slice(0, block * rows)
        for head in range(cols // HEAD_DIM):
            lane = slice(head * HEAD_DIM, (head + 1) * HEAD_DIM)
            k_lane = slice(cols + lane.start, cols + lane.stop)
            v_lane = slice(2 * cols + lane.start, 2 * cols + lane.stop)
            q = qkv[own, lane]
            near = jnp.where(below, scored(q, qkv[own, k_lane]), -1e30)
            top = jnp.max(near, axis=1, keepdims=True)
            if block:
                far = scored(q, qkv[past, k_lane])
                top = jnp.maximum(top, jnp.max(far, axis=1, keepdims=True))
            top = top * factor
            expo = jnp.exp2(near * factor - top)
            bottom = jnp.sum(expo, axis=1, keepdims=True)
            numer = jnp.dot(expo.astype(jnp.bfloat16), qkv[own, v_lane], preferred_element_type=jnp.float32)
            if block:
                expo = jnp.exp2(far * factor - top)
                bottom += jnp.sum(expo, axis=1, keepdims=True)
                numer += jnp.dot(
                    expo.astype(jnp.bfloat16), qkv[past, v_lane], preferred_element_type=jnp.float32
                )
            result[block ^ me, :, lane] = (numer / bottom).astype(jnp.bfloat16)


def join_kernel(cols, total, splits, order, *refs):
    out = refs[-1]
    d, c = lax.axis_index("dp"), lax.axis_index("ctx")
    group = d % 2
    for part, (first_head, heads) in enumerate(splits):
        own, *pieces = refs[part * (total + 1) : (part + 1) * (total + 1)]
        for piece, k in zip(pieces, order):
            base = c ^ k
            same = base // 2 == group
            plane = jnp.where(same, base, base ^ 2)
            core = jnp.where(same, group, 1 - group)
            first = (2 * (plane % 2) + core) * cols + first_head * HEAD_DIM
            lane = pl.ds(pl.multiple_of(first, HEAD_DIM), heads * HEAD_DIM)
            if k:
                out[0, :, lane] = piece[...]
            else:
                out[0, :, lane] = jnp.where(c // 2 == group, own[...], piece[...])


def fast(dp, ctx, tokens, norm_gain, q_weight, k_weight, v_weight):
    rows, features = tokens.shape[1], tokens.shape[2]
    cols = HEADS // ctx * HEAD_DIM
    depth = q_weight.shape[0]
    every = [(d, c) for d in range(dp) for c in range(ctx)]
    plan = PLAN

    def home(to):
        return lambda d, c: to(d, c) if c // 2 == d % 2 else None

    def away(to):
        return lambda d, c: to(d, c) if c // 2 != d % 2 else None

    shift = lambda k: lambda d, c: (d ^ k, c)
    plane = lambda k: lambda d, c: (d, c ^ k)
    routes = {
        "w1": ("o", shift(1)),
        "w2": ("m", shift(2)),
        "w4": ("m", shift(4)),
        "w6": ("w2", shift(4)),
        "w7": ("w5", shift(2)),
        "t1": ("own", home(plane(1))),
        "t2": ("own", away(plane(2))),
        "u0": ("own", home(shift(1))),
        "u1": ("t1", home(shift(1))),
        "u2": ("t2", home(shift(1))),
        "u3": ("t3", home(shift(1))),
    }
    routes["t3"] = ("own", away(plane(3))) if plan["direct3"] else ("t2", home(plane(1)))
    routes["w3"] = ("o", shift(3)) if plan["cross3"] else ("w1", shift(2))
    routes["w5"] = ("o", shift(5)) if plan["cross5"] else ("w1", shift(4))

    d, c = lax.axis_index("dp"), lax.axis_index("ctx")

    def columns(heads):
        return jnp.concatenate(
            [lax.dynamic_slice_in_dim(w, heads * cols, cols, 1) for w in (q_weight, k_weight, v_weight)],
            axis=1,
        )

    heads = 2 * (c % 2) + d % 2
    values = {"own": tokens[0], "o": columns(heads ^ 1), "m": columns(heads)}
    values["cos"], values["sin"] = tables(ctx * rows)
    waits = {name: list(earlier) for name, earlier in plan["waits"]}

    for name in plan["order"]:
        source, to = routes[name]
        operand = values[source]
        earlier = waits.get(name, [])
        if earlier:
            operand, *late = lax.optimization_barrier((operand, *[values[e] for e in earlier]))
            values.update(zip(earlier, late))
        perm = [
            (dd * ctx + cc, to(dd, cc)[0] * ctx + to(dd, cc)[1])
            for dd, cc in every
            if to(dd, cc) is not None
        ]
        with jax.named_scope(name):
            values[name] = lax.ppermute(operand, ("dp", "ctx"), perm)
    cosine, sine = values["cos"], values["sin"]
    names = {0: "m", 1: "w1", 2: "w2", 3: "w3", 4: "w4", 5: "w5", 6: "w6", 7: "w7"}
    early = plan["early"]
    shard_order = early + [k for k in range(8) if k not in early]
    kept = [values[n] for n in ("own", "t1", "t2", "t3")]
    sent = [values[n] for n in ("u0", "u1", "u2", "u3")]

    gain = norm_gain[None, :]
    any_space = pl.BlockSpec(memory_space=pl.ANY)
    vmem = pl.BlockSpec(memory_space=pltpu.VMEM)
    n, late = len(early), 8 - len(early)
    length = ctx * rows
    normed, first = pl.pallas_call(
        functools.partial(norm_kernel, rows, shard_order),
        out_shape=[
            jax.ShapeDtypeStruct((length, features), jnp.bfloat16),
            jax.ShapeDtypeStruct((4 * depth, 3 * cols), jnp.bfloat16),
        ],
        in_specs=[any_space] * 12 + [vmem],
        out_specs=[vmem] * 2,
        scratch_shapes=[
            pltpu.VMEM((length, features), jnp.bfloat16),
            pltpu.SemaphoreType.DMA((4,)),
            pltpu.SemaphoreType.DMA((4,)),
        ],
        compiler_params=pltpu.CompilerParams(vmem_limit_bytes=VMEM_LIMIT),
        cost_estimate=pl.CostEstimate(
            flops=plan["norm_flops"], bytes_accessed=1_000_000, transcendentals=0
        ),
        name="normalize",
    )(*kept, *sent, *[values[names[k]] for k in early[:4]], gain)
    partial = pl.pallas_call(
        early_kernel,
        out_shape=jax.ShapeDtypeStruct((length, 3 * cols), jnp.float32),
        in_specs=[vmem] * 2 + [any_space] * (n - 4),
        out_specs=vmem,
        scratch_shapes=[
            pltpu.VMEM(((n - 4) * depth, 3 * cols), jnp.bfloat16),
            pltpu.SemaphoreType.DMA((n - 4,)),
        ],
        compiler_params=pltpu.CompilerParams(vmem_limit_bytes=VMEM_LIMIT),
        cost_estimate=pl.CostEstimate(
            flops=plan["early_flops"], bytes_accessed=1_000_000, transcendentals=0
        ),
        name="project_early",
    )(normed, first, *[values[names[k]] for k in early[4:]])

    def back(k):
        def to(d, c):
            base = c if c // 2 == d % 2 else c ^ 2
            target = ((d & 6) | (c // 2), base ^ k)
            return None if target == (d, c) else target

        return to

    arrived = []
    last = [values[names[k]] for k in shard_order[n:]]
    for part, (first_head, count) in enumerate(plan["splits"]):
        width = count * HEAD_DIM
        pieces = pl.pallas_call(
            functools.partial(late_kernel, rows, cols, ctx, late, first_head, count),
            out_shape=[jax.ShapeDtypeStruct((rows, width), jnp.bfloat16)] * ctx,
            in_specs=[any_space] * late + [vmem] * 4,
            out_specs=[any_space] * ctx,
            scratch_shapes=[
                pltpu.VMEM((late * depth, 3 * width), jnp.bfloat16),
                pltpu.VMEM((ctx * rows, 3 * width), jnp.bfloat16),
                pltpu.VMEM((ctx, rows, width), jnp.bfloat16),
                pltpu.SemaphoreType.DMA((3 * late,)),
                pltpu.SemaphoreType.DMA((ctx,)),
            ],
            compiler_params=pltpu.CompilerParams(vmem_limit_bytes=VMEM_LIMIT),
            cost_estimate=pl.CostEstimate(
                flops=plan["late_flops"], bytes_accessed=1_000_000, transcendentals=0
            ),
            name=f"attend_{part}",
        )(*last, partial, normed, cosine, sine)
        if arrived:
            hold = plan["hold"]
            both = lax.optimization_barrier((*[arrived[-ctx + k] for k in hold], *pieces))
            for k, value in zip(hold, both):
                arrived[-ctx + k] = value
            pieces = both[len(hold) :]
        elif len(plan["splits"]) > 1:
            pieces = list(pieces)
            pieces[0], last[0] = lax.optimization_barrier((pieces[0], last[0]))
        moved = {}
        for k in plan["back"]:
            with jax.named_scope(f"back_{part}_{k}"):
                to = back(k)
                perm = [
                    (dd * ctx + cc, to(dd, cc)[0] * ctx + to(dd, cc)[1])
                    for dd, cc in every
                    if to(dd, cc) is not None
                ]
                moved[k] = lax.ppermute(pieces[k], ("dp", "ctx"), perm)
        arrived += [pieces[0]] + [moved[k] for k in plan["join"]]
    return pl.pallas_call(
        functools.partial(join_kernel, cols, ctx, plan["splits"], plan["join"]),
        out_shape=jax.ShapeDtypeStruct((1, rows, ctx * cols), jnp.bfloat16),
        in_specs=[vmem] * len(arrived),
        out_specs=vmem,
        compiler_params=pltpu.CompilerParams(vmem_limit_bytes=8 * 1024 * 1024),
        name="join",
    )(*arrived)


def rotate(values, positions):
    heads = values.shape[1] // HEAD_DIM
    shaped = values.reshape(values.shape[0], heads, HEAD_DIM)
    freqs = 10000.0 ** (-(jnp.arange(HALF).astype(jnp.float32) * 2.0) / HEAD_DIM)
    angles = positions[:, None] * freqs[None, :]
    cosine = jnp.cos(angles)[:, None, :]
    sine = jnp.sin(angles)[:, None, :]
    first = shaped[:, :, :HALF]
    second = shaped[:, :, HALF:]
    return jnp.concatenate(
        [first * cosine - second * sine, second * cosine + first * sine], axis=2
    )


def general(dp, ctx, tokens, norm_gain, q_weight, k_weight, v_weight):
    rows = tokens.shape[1]
    heads = HEADS // ctx
    cols = heads * HEAD_DIM
    me = lax.axis_index("ctx")
    part = jnp.concatenate(
        [lax.dynamic_slice_in_dim(w, me * cols, cols, 1) for w in (q_weight, k_weight, v_weight)], axis=1
    )
    weights = lax.all_gather(part, "dp", axis=0, tiled=True)
    whole = lax.all_gather(tokens[0], "ctx", axis=0, tiled=True)
    normed = normalize(whole, norm_gain[None, :])
    linear = jnp.dot(normed, weights, preferred_element_type=jnp.float32)
    length = ctx * rows
    positions = jnp.arange(length).astype(jnp.float32)
    q = rotate(linear[:, :cols], positions).astype(jnp.bfloat16)
    k = rotate(linear[:, cols : 2 * cols], positions).astype(jnp.bfloat16)
    v = linear[:, 2 * cols :].astype(jnp.bfloat16).reshape(length, heads, HEAD_DIM)
    allowed = jnp.arange(length)[None, :] <= jnp.arange(length)[:, None]
    scores = jnp.einsum("qhd,khd->hqk", q, k, preferred_element_type=jnp.float32) * HEAD_DIM ** (-0.5)
    scores = jnp.where(allowed[None], scores, -1e30)
    top = jnp.max(scores, axis=2, keepdims=True)
    expo = jnp.where(allowed[None], jnp.exp(scores - top), 0.0)
    numer = jnp.einsum("hqk,khd->hqd", expo.astype(jnp.bfloat16), v, preferred_element_type=jnp.float32)
    result = (numer / jnp.sum(expo, axis=2, keepdims=True)).astype(jnp.bfloat16)
    result = result.reshape(heads, ctx, rows, HEAD_DIM).transpose(1, 2, 0, 3).reshape(ctx, rows, cols)
    back = lax.all_to_all(result, "ctx", 0, 0)
    return back.transpose(1, 0, 2).reshape(1, rows, ctx * cols)


def solution(mesh):
    dp, ctx = mesh.shape["dp"], mesh.shape["ctx"]
    body = fast if (dp, ctx) == (8, 4) else general
    placed = (P("dp", "ctx", None), P(), P("dp", None), P("dp", None), P("dp", None))
    return jax.shard_map(
        functools.partial(body, dp, ctx),
        mesh=mesh,
        in_specs=placed,
        out_specs=P("dp", "ctx", None),
        check_vma=False,
    )
```

```python
import functools
import math

import jax
import jax.numpy as jnp
from jax import lax
from jax.experimental import pallas as pl
from jax.experimental.pallas import tpu as pltpu
from jax.sharding import PartitionSpec as P

HEADS = 16
HEAD_DIM = 128
HALF = HEAD_DIM // 2
EPS = 1e-05
VMEM_LIMIT = 28 * 1024 * 1024

PLAN = {
    "order": ["t2", "w1", "u0", "w2", "w5", "w7", "t3", "u2", "w3", "u3", "t1", "w6", "u1", "w4"],
    "waits": [["w6", ["t1", "u0"]], ["w7", ["w2"]], ["t3", ["w2"]], ["w4", ["u1", "u2"]], ["t1", ["cos", "sin"]]],
    "early": [0, 1, 2, 5, 6, 7],
    "splits": [[0, 4]],
    "hold": [0, 1, 2, 3],
    "back": [1, 0, 3, 2],
    "direct3": False,
    "cross3": False,
    "cross5": False,
    "early_flops": 4000000000,
    "late_flops": 1000000,
    "norm_flops": 4000000000,
    "join": [1, 0, 3, 2],
}


def tables(length):
    freqs = 10000.0 ** (-(jnp.arange(HALF).astype(jnp.float32) * 2.0) / HEAD_DIM)
    angles = jnp.arange(length).astype(jnp.float32)[:, None] * freqs[None, :]
    cosine = jnp.cos(angles)
    sine = jnp.sin(angles)
    return (
        jnp.concatenate([cosine, cosine], axis=1),
        jnp.concatenate([-sine, sine], axis=1),
    )


def normalize(block, gain):
    rows = block.astype(jnp.float32)
    scale = lax.rsqrt(jnp.mean(rows * rows, axis=1, keepdims=True) + EPS)
    return (rows * scale * gain.astype(jnp.float32)).astype(jnp.bfloat16)


def role(rows):
    d, c = lax.axis_index("dp"), lax.axis_index("ctx")
    home = c // 2 == d % 2
    return {
        "home": home,
        "starts": [pl.multiple_of((c ^ i) * rows, rows) for i in range(4)],
        "base": jnp.where(home, c, c ^ 2),
        "owner": d,
    }


def norm_kernel(rows, order, *refs):
    kept, sent, shards = refs[:4], refs[4:8], refs[8:12]
    gain, out, weights, held, token_sems, weight_sems = refs[12:]
    me = role(rows)
    depth = shards[0].shape[0]
    loads = []
    for i in range(4):
        slot = held.at[pl.ds(i * rows, rows)]
        for condition, source in ((me["home"], kept[i]), (jnp.logical_not(me["home"]), sent[i])):

            @pl.when(condition)
            def _(source=source, slot=slot, i=i):
                pltpu.make_async_copy(source, slot, token_sems.at[i]).start()

        loads.append(pltpu.make_async_copy(kept[i], slot, token_sems.at[i]))
    weight_loads = []
    for i, shard in enumerate(shards):
        load = pltpu.make_async_copy(shard, weights.at[pl.ds(i * depth, depth)], weight_sems.at[i])
        load.start()
        weight_loads.append(load)
    lanes = []
    for owner in range(8):
        offset = me["owner"] ^ owner
        place = sum(jnp.where(offset == k, at, 0) for at, k in enumerate(order))
        lanes.append(pl.ds(pl.multiple_of(place * depth, depth), depth))
    for i in range(4):
        loads[i].wait()
        part = pl.ds(i * rows, rows)
        value = normalize(held[part, :], gain[...])
        for owner, lane in enumerate(lanes):
            out[part, lane] = value[:, owner * depth : (owner + 1) * depth]
    for load in weight_loads:
        load.wait()


def load_shards(shards, weights, sems, lanes):
    depth = shards[0].shape[0]
    loads = []
    for i, shard in enumerate(shards):
        for j, (source, target, width) in enumerate(lanes):
            load = pltpu.make_async_copy(
                shard.at[:, pl.ds(source, width)],
                weights.at[pl.ds(i * depth, depth), pl.ds(target, width)],
                sems.at[len(lanes) * i + j],
            )
            load.start()
            loads.append(load)
    return loads


def early_kernel(*refs):
    normed, first, shards, out, weights, sems = refs[0], refs[1], refs[2:-3], *refs[-3:]
    columns = out.shape[1]
    loads = load_shards(shards, weights, sems, [(0, 0, columns)])
    for load in loads:
        load.wait()
    middle, end = first.shape[0], first.shape[0] + weights.shape[0]
    step = 2 * HEAD_DIM
    for lane in range(0, columns, step):
        lanes = slice(lane, lane + step)
        out[:, lanes] = jnp.dot(
            normed[:, :middle], first[:, lanes], preferred_element_type=jnp.float32
        ) + jnp.dot(normed[:, middle:end], weights[:, lanes], preferred_element_type=jnp.float32)


def late_kernel(rows, cols, total, count, first_head, heads, *refs):
    shards = refs[:count]
    partial, normed, cos_ref, sin_ref = refs[count : count + 4]
    outs = refs[count + 4 : count + 4 + total]
    qkv, result, out_sems = refs[count + 4 + total :]
    me = role(rows)
    width = heads * HEAD_DIM
    start_lane = first_head * HEAD_DIM
    depth = shards[0].shape[0]
    tail = normed.shape[1] - count * depth
    step = HEAD_DIM if width % (2 * HEAD_DIM) else 2 * HEAD_DIM
    for j in range(3):
        for lane in range(0, width, step):
            first = j * cols + start_lane + lane
            linear = partial[:, first : first + step]
            for i, shard in enumerate(shards):
                linear += jnp.dot(
                    normed[:, tail + i * depth : tail + (i + 1) * depth],
                    shard[:, first : first + step],
                    preferred_element_type=jnp.float32,
                )
            for i, start in enumerate(me["starts"]):
                value = linear[i * rows : (i + 1) * rows]
                if j < 2:
                    cosine = cos_ref[pl.ds(start, rows), :]
                    sine = sin_ref[pl.ds(start, rows), :]
                    parts = [value[:, h * HEAD_DIM : (h + 1) * HEAD_DIM] for h in range(step // HEAD_DIM)]
                    value = jnp.concatenate(
                        [x * cosine + pltpu.roll(x, HALF, 1) * sine for x in parts], axis=1
                    )
                lanes = slice(j * width + lane, j * width + lane + step)
                qkv[pl.ds(start, rows), lanes] = value.astype(jnp.bfloat16)
    attend(qkv, result, me["base"], total, rows, width)
    copies = []
    for k in range(total):
        copy = pltpu.make_async_copy(result.at[k], outs[k], out_sems.at[k])
        copy.start()
        copies.append(copy)
    for copy in copies:
        copy.wait()


def attend(qkv, result, me, total, rows, cols):
    factor = HEAD_DIM ** (-0.5) * math.log2(math.e)
    below = lax.broadcasted_iota(jnp.int32, (rows, rows), 0) >= lax.broadcasted_iota(
        jnp.int32, (rows, rows), 1
    )

    def scored(q, k):
        return lax.dot_general(q, k, (((1,), (1,)), ((), ())), preferred_element_type=jnp.float32)

    for block in range(total):
        own, past = slice(block * rows, (block + 1) * rows), slice(0, block * rows)
        for head in range(cols // HEAD_DIM):
            lane = slice(head * HEAD_DIM, (head + 1) * HEAD_DIM)
            k_lane = slice(cols + lane.start, cols + lane.stop)
            v_lane = slice(2 * cols + lane.start, 2 * cols + lane.stop)
            q = qkv[own, lane]
            near = jnp.where(below, scored(q, qkv[own, k_lane]), -1e30)
            top = jnp.max(near, axis=1, keepdims=True)
            if block:
                far = scored(q, qkv[past, k_lane])
                top = jnp.maximum(top, jnp.max(far, axis=1, keepdims=True))
            top = top * factor
            expo = jnp.exp2(near * factor - top)
            bottom = jnp.sum(expo, axis=1, keepdims=True)
            numer = jnp.dot(expo.astype(jnp.bfloat16), qkv[own, v_lane], preferred_element_type=jnp.float32)
            if block:
                expo = jnp.exp2(far * factor - top)
                bottom += jnp.sum(expo, axis=1, keepdims=True)
                numer += jnp.dot(
                    expo.astype(jnp.bfloat16), qkv[past, v_lane], preferred_element_type=jnp.float32
                )
            result[block ^ me, :, lane] = (numer / bottom).astype(jnp.bfloat16)


def join_kernel(cols, total, splits, order, *refs):
    out = refs[-1]
    d, c = lax.axis_index("dp"), lax.axis_index("ctx")
    group = d % 2
    for part, (first_head, heads) in enumerate(splits):
        own, *pieces = refs[part * (total + 1) : (part + 1) * (total + 1)]
        for piece, k in zip(pieces, order):
            base = c ^ k
            same = base // 2 == group
            plane = jnp.where(same, base, base ^ 2)
            core = jnp.where(same, group, 1 - group)
            first = (2 * (plane % 2) + core) * cols + first_head * HEAD_DIM
            lane = pl.ds(pl.multiple_of(first, HEAD_DIM), heads * HEAD_DIM)
            if k:
                out[0, :, lane] = piece[...]
            else:
                out[0, :, lane] = jnp.where(c // 2 == group, own[...], piece[...])


def fast(dp, ctx, tokens, norm_gain, q_weight, k_weight, v_weight):
    rows, features = tokens.shape[1], tokens.shape[2]
    cols = HEADS // ctx * HEAD_DIM
    depth = q_weight.shape[0]
    every = [(d, c) for d in range(dp) for c in range(ctx)]
    plan = PLAN

    def home(to):
        return lambda d, c: to(d, c) if c // 2 == d % 2 else None

    def away(to):
        return lambda d, c: to(d, c) if c // 2 != d % 2 else None

    shift = lambda k: lambda d, c: (d ^ k, c)
    plane = lambda k: lambda d, c: (d, c ^ k)
    routes = {
        "w1": ("o", shift(1)),
        "w2": ("m", shift(2)),
        "w4": ("m", shift(4)),
        "w6": ("w2", shift(4)),
        "w7": ("w5", shift(2)),
        "t1": ("own", home(plane(1))),
        "t2": ("own", away(plane(2))),
        "u0": ("own", home(shift(1))),
        "u1": ("t1", home(shift(1))),
        "u2": ("t2", home(shift(1))),
        "u3": ("t3", home(shift(1))),
    }
    routes["t3"] = ("own", away(plane(3))) if plan["direct3"] else ("t2", home(plane(1)))
    routes["w3"] = ("o", shift(3)) if plan["cross3"] else ("w1", shift(2))
    routes["w5"] = ("o", shift(5)) if plan["cross5"] else ("w1", shift(4))

    d, c = lax.axis_index("dp"), lax.axis_index("ctx")

    def columns(heads):
        return jnp.concatenate(
            [lax.dynamic_slice_in_dim(w, heads * cols, cols, 1) for w in (q_weight, k_weight, v_weight)],
            axis=1,
        )

    heads = 2 * (c % 2) + d % 2
    values = {"own": tokens[0], "o": columns(heads ^ 1), "m": columns(heads)}
    values["cos"], values["sin"] = tables(ctx * rows)
    waits = {name: list(earlier) for name, earlier in plan["waits"]}

    for name in plan["order"]:
        source, to = routes[name]
        operand = values[source]
        earlier = waits.get(name, [])
        if earlier:
            operand, *late = lax.optimization_barrier((operand, *[values[e] for e in earlier]))
            values.update(zip(earlier, late))
        perm = [
            (dd * ctx + cc, to(dd, cc)[0] * ctx + to(dd, cc)[1])
            for dd, cc in every
            if to(dd, cc) is not None
        ]
        with jax.named_scope(name):
            values[name] = lax.ppermute(operand, ("dp", "ctx"), perm)
    cosine, sine = values["cos"], values["sin"]
    names = {0: "m", 1: "w1", 2: "w2", 3: "w3", 4: "w4", 5: "w5", 6: "w6", 7: "w7"}
    early = plan["early"]
    shard_order = early + [k for k in range(8) if k not in early]
    kept = [values[n] for n in ("own", "t1", "t2", "t3")]
    sent = [values[n] for n in ("u0", "u1", "u2", "u3")]

    gain = norm_gain[None, :]
    any_space = pl.BlockSpec(memory_space=pl.ANY)
    vmem = pl.BlockSpec(memory_space=pltpu.VMEM)
    n, late = len(early), 8 - len(early)
    length = ctx * rows
    normed, first = pl.pallas_call(
        functools.partial(norm_kernel, rows, shard_order),
        out_shape=[
            jax.ShapeDtypeStruct((length, features), jnp.bfloat16),
            jax.ShapeDtypeStruct((4 * depth, 3 * cols), jnp.bfloat16),
        ],
        in_specs=[any_space] * 12 + [vmem],
        out_specs=[vmem] * 2,
        scratch_shapes=[
            pltpu.VMEM((length, features), jnp.bfloat16),
            pltpu.SemaphoreType.DMA((4,)),
            pltpu.SemaphoreType.DMA((4,)),
        ],
        compiler_params=pltpu.CompilerParams(vmem_limit_bytes=VMEM_LIMIT),
        cost_estimate=pl.CostEstimate(
            flops=plan["norm_flops"], bytes_accessed=1_000_000, transcendentals=0
        ),
        name="normalize",
    )(*kept, *sent, *[values[names[k]] for k in early[:4]], gain)
    partial = pl.pallas_call(
        early_kernel,
        out_shape=jax.ShapeDtypeStruct((length, 3 * cols), jnp.float32),
        in_specs=[vmem] * 2 + [any_space] * (n - 4),
        out_specs=vmem,
        scratch_shapes=[
            pltpu.VMEM(((n - 4) * depth, 3 * cols), jnp.bfloat16),
            pltpu.SemaphoreType.DMA((n - 4,)),
        ],
        compiler_params=pltpu.CompilerParams(vmem_limit_bytes=VMEM_LIMIT),
        cost_estimate=pl.CostEstimate(
            flops=plan["early_flops"], bytes_accessed=1_000_000, transcendentals=0
        ),
        name="project_early",
    )(normed, first, *[values[names[k]] for k in early[4:]])

    def back(k):
        def to(d, c):
            base = c if c // 2 == d % 2 else c ^ 2
            target = ((d & 6) | (c // 2), base ^ k)
            return None if target == (d, c) else target

        return to

    arrived = []
    last = [values[names[k]] for k in shard_order[n:]]
    for part, (first_head, count) in enumerate(plan["splits"]):
        width = count * HEAD_DIM
        pieces = pl.pallas_call(
            functools.partial(late_kernel, rows, cols, ctx, late, first_head, count),
            out_shape=[jax.ShapeDtypeStruct((rows, width), jnp.bfloat16)] * ctx,
            in_specs=[vmem] * (late + 4),
            out_specs=[any_space] * ctx,
            scratch_shapes=[
                pltpu.VMEM((ctx * rows, 3 * width), jnp.bfloat16),
                pltpu.VMEM((ctx, rows, width), jnp.bfloat16),
                pltpu.SemaphoreType.DMA((ctx,)),
            ],
            compiler_params=pltpu.CompilerParams(vmem_limit_bytes=VMEM_LIMIT),
            cost_estimate=pl.CostEstimate(
                flops=plan["late_flops"], bytes_accessed=1_000_000, transcendentals=0
            ),
            name=f"attend_{part}",
        )(*last, partial, normed, cosine, sine)
        if arrived:
            hold = plan["hold"]
            both = lax.optimization_barrier((*[arrived[-ctx + k] for k in hold], *pieces))
            for k, value in zip(hold, both):
                arrived[-ctx + k] = value
            pieces = both[len(hold) :]
        elif len(plan["splits"]) > 1:
            pieces = list(pieces)
            pieces[0], last[0] = lax.optimization_barrier((pieces[0], last[0]))
        moved = {}
        for k in plan["back"]:
            with jax.named_scope(f"back_{part}_{k}"):
                to = back(k)
                perm = [
                    (dd * ctx + cc, to(dd, cc)[0] * ctx + to(dd, cc)[1])
                    for dd, cc in every
                    if to(dd, cc) is not None
                ]
                moved[k] = lax.ppermute(pieces[k], ("dp", "ctx"), perm)
        arrived += [pieces[0]] + [moved[k] for k in plan["join"]]
    return pl.pallas_call(
        functools.partial(join_kernel, cols, ctx, plan["splits"], plan["join"]),
        out_shape=jax.ShapeDtypeStruct((1, rows, ctx * cols), jnp.bfloat16),
        in_specs=[vmem] * len(arrived),
        out_specs=vmem,
        compiler_params=pltpu.CompilerParams(vmem_limit_bytes=8 * 1024 * 1024),
        name="join",
    )(*arrived)


def rotate(values, positions):
    heads = values.shape[1] // HEAD_DIM
    shaped = values.reshape(values.shape[0], heads, HEAD_DIM)
    freqs = 10000.0 ** (-(jnp.arange(HALF).astype(jnp.float32) * 2.0) / HEAD_DIM)
    angles = positions[:, None] * freqs[None, :]
    cosine = jnp.cos(angles)[:, None, :]
    sine = jnp.sin(angles)[:, None, :]
    first = shaped[:, :, :HALF]
    second = shaped[:, :, HALF:]
    return jnp.concatenate(
        [first * cosine - second * sine, second * cosine + first * sine], axis=2
    )


def general(dp, ctx, tokens, norm_gain, q_weight, k_weight, v_weight):
    rows = tokens.shape[1]
    heads = HEADS // ctx
    cols = heads * HEAD_DIM
    me = lax.axis_index("ctx")
    part = jnp.concatenate(
        [lax.dynamic_slice_in_dim(w, me * cols, cols, 1) for w in (q_weight, k_weight, v_weight)], axis=1
    )
    weights = lax.all_gather(part, "dp", axis=0, tiled=True)
    whole = lax.all_gather(tokens[0], "ctx", axis=0, tiled=True)
    normed = normalize(whole, norm_gain[None, :])
    linear = jnp.dot(normed, weights, preferred_element_type=jnp.float32)
    length = ctx * rows
    positions = jnp.arange(length).astype(jnp.float32)
    q = rotate(linear[:, :cols], positions).astype(jnp.bfloat16)
    k = rotate(linear[:, cols : 2 * cols], positions).astype(jnp.bfloat16)
    v = linear[:, 2 * cols :].astype(jnp.bfloat16).reshape(length, heads, HEAD_DIM)
    allowed = jnp.arange(length)[None, :] <= jnp.arange(length)[:, None]
    scores = jnp.einsum("qhd,khd->hqk", q, k, preferred_element_type=jnp.float32) * HEAD_DIM ** (-0.5)
    scores = jnp.where(allowed[None], scores, -1e30)
    top = jnp.max(scores, axis=2, keepdims=True)
    expo = jnp.where(allowed[None], jnp.exp(scores - top), 0.0)
    numer = jnp.einsum("hqk,khd->hqd", expo.astype(jnp.bfloat16), v, preferred_element_type=jnp.float32)
    result = (numer / jnp.sum(expo, axis=2, keepdims=True)).astype(jnp.bfloat16)
    result = result.reshape(heads, ctx, rows, HEAD_DIM).transpose(1, 2, 0, 3).reshape(ctx, rows, cols)
    back = lax.all_to_all(result, "ctx", 0, 0)
    return back.transpose(1, 0, 2).reshape(1, rows, ctx * cols)


def solution(mesh):
    dp, ctx = mesh.shape["dp"], mesh.shape["ctx"]
    body = fast if (dp, ctx) == (8, 4) else general
    placed = (P("dp", "ctx", None), P(), P("dp", None), P("dp", None), P("dp", None))
    return jax.shard_map(
        functools.partial(body, dp, ctx),
        mesh=mesh,
        in_specs=placed,
        out_specs=P("dp", "ctx", None),
        check_vma=False,
    )
```

```python
import functools
import math

import jax
import jax.numpy as jnp
from jax import lax
from jax.experimental import pallas as pl
from jax.experimental.pallas import tpu as pltpu
from jax.sharding import PartitionSpec as P

HEADS = 16
HEAD_DIM = 128
HALF = HEAD_DIM // 2
EPS = 1e-05
VMEM_LIMIT = 28 * 1024 * 1024

PLAN = {
    "order": ["t2", "w1", "u0", "w2", "w5", "w7", "t3", "u2", "w3", "u3", "t1", "w6", "u1", "w4"],
    "waits": [["w6", ["t1", "u0"]], ["w7", ["w2"]], ["t3", ["w2"]], ["w4", ["u1", "u2"]], ["t1", ["cos", "sin"]]],
    "early": [0, 1, 2, 5, 6, 7],
    "splits": [[0, 4]],
    "hold": [0, 1, 2, 3],
    "back": [1, 0, 3, 2],
    "direct3": False,
    "cross3": False,
    "cross5": False,
    "early_flops": 4000000000,
    "late_flops": 1000000,
    "norm_flops": 4000000000,
    "join": [1, 0, 3, 2],
}


def tables(length):
    freqs = 10000.0 ** (-(jnp.arange(HALF).astype(jnp.float32) * 2.0) / HEAD_DIM)
    angles = jnp.arange(length).astype(jnp.float32)[:, None] * freqs[None, :]
    cosine = jnp.cos(angles)
    sine = jnp.sin(angles)
    return (
        jnp.concatenate([cosine, cosine], axis=1),
        jnp.concatenate([-sine, sine], axis=1),
    )


def normalize(block, gain):
    rows = block.astype(jnp.float32)
    scale = lax.rsqrt(jnp.mean(rows * rows, axis=1, keepdims=True) + EPS)
    return (rows * scale * gain.astype(jnp.float32)).astype(jnp.bfloat16)


def role(rows):
    d, c = lax.axis_index("dp"), lax.axis_index("ctx")
    home = c // 2 == d % 2
    return {
        "home": home,
        "starts": [pl.multiple_of((c ^ i) * rows, rows) for i in range(4)],
        "base": jnp.where(home, c, c ^ 2),
        "owner": d,
    }


def norm_kernel(rows, order, *refs):
    kept, sent, shards = refs[:4], refs[4:8], refs[8:12]
    gain, out, weights, held, token_sems, weight_sems = refs[12:]
    me = role(rows)
    depth = shards[0].shape[0]
    loads = []
    for i in range(4):
        slot = held.at[pl.ds(i * rows, rows)]
        for condition, source in ((me["home"], kept[i]), (jnp.logical_not(me["home"]), sent[i])):

            @pl.when(condition)
            def _(source=source, slot=slot, i=i):
                pltpu.make_async_copy(source, slot, token_sems.at[i]).start()

        loads.append(pltpu.make_async_copy(kept[i], slot, token_sems.at[i]))
    weight_loads = []
    for i, shard in enumerate(shards):
        load = pltpu.make_async_copy(shard, weights.at[pl.ds(i * depth, depth)], weight_sems.at[i])
        load.start()
        weight_loads.append(load)
    lanes = []
    for owner in range(8):
        offset = me["owner"] ^ owner
        place = sum(jnp.where(offset == k, at, 0) for at, k in enumerate(order))
        lanes.append(pl.ds(pl.multiple_of(place * depth, depth), depth))
    for i in range(4):
        loads[i].wait()
        part = pl.ds(i * rows, rows)
        value = normalize(held[part, :], gain[...])
        for owner, lane in enumerate(lanes):
            out[part, lane] = value[:, owner * depth : (owner + 1) * depth]
    for load in weight_loads:
        load.wait()


def load_shards(shards, weights, sems, lanes):
    depth = shards[0].shape[0]
    loads = []
    for i, shard in enumerate(shards):
        for j, (source, target, width) in enumerate(lanes):
            load = pltpu.make_async_copy(
                shard.at[:, pl.ds(source, width)],
                weights.at[pl.ds(i * depth, depth), pl.ds(target, width)],
                sems.at[len(lanes) * i + j],
            )
            load.start()
            loads.append(load)
    return loads


def early_kernel(*refs):
    normed, first, shards, out = refs[0], refs[1], refs[2:-1], refs[-1]
    step = 2 * HEAD_DIM
    for lane in range(0, out.shape[1], step):
        lanes = slice(lane, lane + step)
        row = first.shape[0]
        total = jnp.dot(normed[:, :row], first[:, lanes], preferred_element_type=jnp.float32)
        for shard in shards:
            end = row + shard.shape[0]
            total += jnp.dot(normed[:, row:end], shard[:, lanes], preferred_element_type=jnp.float32)
            row = end
        out[:, lanes] = total


def late_kernel(rows, cols, total, count, first_head, heads, *refs):
    shards = refs[:count]
    partial, normed, cos_ref, sin_ref = refs[count : count + 4]
    outs = refs[count + 4 : count + 4 + total]
    qkv, result, out_sems = refs[count + 4 + total :]
    me = role(rows)
    width = heads * HEAD_DIM
    start_lane = first_head * HEAD_DIM
    depth = shards[0].shape[0]
    tail = normed.shape[1] - count * depth
    step = HEAD_DIM if width % (2 * HEAD_DIM) else 2 * HEAD_DIM
    for j in range(3):
        for lane in range(0, width, step):
            first = j * cols + start_lane + lane
            linear = partial[:, first : first + step]
            for i, shard in enumerate(shards):
                linear += jnp.dot(
                    normed[:, tail + i * depth : tail + (i + 1) * depth],
                    shard[:, first : first + step],
                    preferred_element_type=jnp.float32,
                )
            for i, start in enumerate(me["starts"]):
                value = linear[i * rows : (i + 1) * rows]
                if j < 2:
                    cosine = cos_ref[pl.ds(start, rows), :]
                    sine = sin_ref[pl.ds(start, rows), :]
                    parts = [value[:, h * HEAD_DIM : (h + 1) * HEAD_DIM] for h in range(step // HEAD_DIM)]
                    value = jnp.concatenate(
                        [x * cosine + pltpu.roll(x, HALF, 1) * sine for x in parts], axis=1
                    )
                lanes = slice(j * width + lane, j * width + lane + step)
                qkv[pl.ds(start, rows), lanes] = value.astype(jnp.bfloat16)
    attend(qkv, result, me["base"], total, rows, width)
    copies = []
    for k in range(total):
        copy = pltpu.make_async_copy(result.at[k], outs[k], out_sems.at[k])
        copy.start()
        copies.append(copy)
    for copy in copies:
        copy.wait()


def attend(qkv, result, me, total, rows, cols):
    factor = HEAD_DIM ** (-0.5) * math.log2(math.e)
    below = lax.broadcasted_iota(jnp.int32, (rows, rows), 0) >= lax.broadcasted_iota(
        jnp.int32, (rows, rows), 1
    )

    def scored(q, k):
        return lax.dot_general(q, k, (((1,), (1,)), ((), ())), preferred_element_type=jnp.float32)

    for block in range(total):
        own, past = slice(block * rows, (block + 1) * rows), slice(0, block * rows)
        for head in range(cols // HEAD_DIM):
            lane = slice(head * HEAD_DIM, (head + 1) * HEAD_DIM)
            k_lane = slice(cols + lane.start, cols + lane.stop)
            v_lane = slice(2 * cols + lane.start, 2 * cols + lane.stop)
            q = qkv[own, lane]
            near = jnp.where(below, scored(q, qkv[own, k_lane]), -1e30)
            top = jnp.max(near, axis=1, keepdims=True)
            if block:
                far = scored(q, qkv[past, k_lane])
                top = jnp.maximum(top, jnp.max(far, axis=1, keepdims=True))
            top = top * factor
            expo = jnp.exp2(near * factor - top)
            bottom = jnp.sum(expo, axis=1, keepdims=True)
            numer = jnp.dot(expo.astype(jnp.bfloat16), qkv[own, v_lane], preferred_element_type=jnp.float32)
            if block:
                expo = jnp.exp2(far * factor - top)
                bottom += jnp.sum(expo, axis=1, keepdims=True)
                numer += jnp.dot(
                    expo.astype(jnp.bfloat16), qkv[past, v_lane], preferred_element_type=jnp.float32
                )
            result[block ^ me, :, lane] = (numer / bottom).astype(jnp.bfloat16)


def join_kernel(cols, total, splits, order, *refs):
    out = refs[-1]
    d, c = lax.axis_index("dp"), lax.axis_index("ctx")
    group = d % 2
    for part, (first_head, heads) in enumerate(splits):
        own, *pieces = refs[part * (total + 1) : (part + 1) * (total + 1)]
        for piece, k in zip(pieces, order):
            base = c ^ k
            same = base // 2 == group
            plane = jnp.where(same, base, base ^ 2)
            core = jnp.where(same, group, 1 - group)
            first = (2 * (plane % 2) + core) * cols + first_head * HEAD_DIM
            lane = pl.ds(pl.multiple_of(first, HEAD_DIM), heads * HEAD_DIM)
            if k:
                out[0, :, lane] = piece[...]
            else:
                out[0, :, lane] = jnp.where(c // 2 == group, own[...], piece[...])


def fast(dp, ctx, tokens, norm_gain, q_weight, k_weight, v_weight):
    rows, features = tokens.shape[1], tokens.shape[2]
    cols = HEADS // ctx * HEAD_DIM
    depth = q_weight.shape[0]
    every = [(d, c) for d in range(dp) for c in range(ctx)]
    plan = PLAN

    def home(to):
        return lambda d, c: to(d, c) if c // 2 == d % 2 else None

    def away(to):
        return lambda d, c: to(d, c) if c // 2 != d % 2 else None

    shift = lambda k: lambda d, c: (d ^ k, c)
    plane = lambda k: lambda d, c: (d, c ^ k)
    routes = {
        "w1": ("o", shift(1)),
        "w2": ("m", shift(2)),
        "w4": ("m", shift(4)),
        "w6": ("w2", shift(4)),
        "w7": ("w5", shift(2)),
        "t1": ("own", home(plane(1))),
        "t2": ("own", away(plane(2))),
        "u0": ("own", home(shift(1))),
        "u1": ("t1", home(shift(1))),
        "u2": ("t2", home(shift(1))),
        "u3": ("t3", home(shift(1))),
    }
    routes["t3"] = ("own", away(plane(3))) if plan["direct3"] else ("t2", home(plane(1)))
    routes["w3"] = ("o", shift(3)) if plan["cross3"] else ("w1", shift(2))
    routes["w5"] = ("o", shift(5)) if plan["cross5"] else ("w1", shift(4))

    d, c = lax.axis_index("dp"), lax.axis_index("ctx")

    def columns(heads):
        return jnp.concatenate(
            [lax.dynamic_slice_in_dim(w, heads * cols, cols, 1) for w in (q_weight, k_weight, v_weight)],
            axis=1,
        )

    heads = 2 * (c % 2) + d % 2
    values = {"own": tokens[0], "o": columns(heads ^ 1), "m": columns(heads)}
    values["cos"], values["sin"] = tables(ctx * rows)
    waits = {name: list(earlier) for name, earlier in plan["waits"]}

    for name in plan["order"]:
        source, to = routes[name]
        operand = values[source]
        earlier = waits.get(name, [])
        if earlier:
            operand, *late = lax.optimization_barrier((operand, *[values[e] for e in earlier]))
            values.update(zip(earlier, late))
        perm = [
            (dd * ctx + cc, to(dd, cc)[0] * ctx + to(dd, cc)[1])
            for dd, cc in every
            if to(dd, cc) is not None
        ]
        with jax.named_scope(name):
            values[name] = lax.ppermute(operand, ("dp", "ctx"), perm)
    cosine, sine = values["cos"], values["sin"]
    names = {0: "m", 1: "w1", 2: "w2", 3: "w3", 4: "w4", 5: "w5", 6: "w6", 7: "w7"}
    early = plan["early"]
    shard_order = early + [k for k in range(8) if k not in early]
    kept = [values[n] for n in ("own", "t1", "t2", "t3")]
    sent = [values[n] for n in ("u0", "u1", "u2", "u3")]

    gain = norm_gain[None, :]
    any_space = pl.BlockSpec(memory_space=pl.ANY)
    vmem = pl.BlockSpec(memory_space=pltpu.VMEM)
    n, late = len(early), 8 - len(early)
    length = ctx * rows
    normed, first = pl.pallas_call(
        functools.partial(norm_kernel, rows, shard_order),
        out_shape=[
            jax.ShapeDtypeStruct((length, features), jnp.bfloat16),
            jax.ShapeDtypeStruct((4 * depth, 3 * cols), jnp.bfloat16),
        ],
        in_specs=[any_space] * 12 + [vmem],
        out_specs=[vmem] * 2,
        scratch_shapes=[
            pltpu.VMEM((length, features), jnp.bfloat16),
            pltpu.SemaphoreType.DMA((4,)),
            pltpu.SemaphoreType.DMA((4,)),
        ],
        compiler_params=pltpu.CompilerParams(vmem_limit_bytes=VMEM_LIMIT),
        cost_estimate=pl.CostEstimate(
            flops=plan["norm_flops"], bytes_accessed=1_000_000, transcendentals=0
        ),
        name="normalize",
    )(*kept, *sent, *[values[names[k]] for k in early[:4]], gain)
    partial = pl.pallas_call(
        early_kernel,
        out_shape=jax.ShapeDtypeStruct((length, 3 * cols), jnp.float32),
        in_specs=[vmem] * (n - 2),
        out_specs=vmem,
        compiler_params=pltpu.CompilerParams(vmem_limit_bytes=VMEM_LIMIT),
        cost_estimate=pl.CostEstimate(
            flops=plan["early_flops"], bytes_accessed=1_000_000, transcendentals=0
        ),
        name="project_early",
    )(normed, first, *[values[names[k]] for k in early[4:]])

    def back(k):
        def to(d, c):
            base = c if c // 2 == d % 2 else c ^ 2
            target = ((d & 6) | (c // 2), base ^ k)
            return None if target == (d, c) else target

        return to

    arrived = []
    last = [values[names[k]] for k in shard_order[n:]]
    for part, (first_head, count) in enumerate(plan["splits"]):
        width = count * HEAD_DIM
        pieces = pl.pallas_call(
            functools.partial(late_kernel, rows, cols, ctx, late, first_head, count),
            out_shape=[jax.ShapeDtypeStruct((rows, width), jnp.bfloat16)] * ctx,
            in_specs=[vmem] * (late + 4),
            out_specs=[any_space] * ctx,
            scratch_shapes=[
                pltpu.VMEM((ctx * rows, 3 * width), jnp.bfloat16),
                pltpu.VMEM((ctx, rows, width), jnp.bfloat16),
                pltpu.SemaphoreType.DMA((ctx,)),
            ],
            compiler_params=pltpu.CompilerParams(vmem_limit_bytes=VMEM_LIMIT),
            cost_estimate=pl.CostEstimate(
                flops=plan["late_flops"], bytes_accessed=1_000_000, transcendentals=0
            ),
            name=f"attend_{part}",
        )(*last, partial, normed, cosine, sine)
        if arrived:
            hold = plan["hold"]
            both = lax.optimization_barrier((*[arrived[-ctx + k] for k in hold], *pieces))
            for k, value in zip(hold, both):
                arrived[-ctx + k] = value
            pieces = both[len(hold) :]
        elif len(plan["splits"]) > 1:
            pieces = list(pieces)
            pieces[0], last[0] = lax.optimization_barrier((pieces[0], last[0]))
        moved = {}
        for k in plan["back"]:
            with jax.named_scope(f"back_{part}_{k}"):
                to = back(k)
                perm = [
                    (dd * ctx + cc, to(dd, cc)[0] * ctx + to(dd, cc)[1])
                    for dd, cc in every
                    if to(dd, cc) is not None
                ]
                moved[k] = lax.ppermute(pieces[k], ("dp", "ctx"), perm)
        arrived += [pieces[0]] + [moved[k] for k in plan["join"]]
    return pl.pallas_call(
        functools.partial(join_kernel, cols, ctx, plan["splits"], plan["join"]),
        out_shape=jax.ShapeDtypeStruct((1, rows, ctx * cols), jnp.bfloat16),
        in_specs=[vmem] * len(arrived),
        out_specs=vmem,
        compiler_params=pltpu.CompilerParams(vmem_limit_bytes=8 * 1024 * 1024),
        name="join",
    )(*arrived)


def rotate(values, positions):
    heads = values.shape[1] // HEAD_DIM
    shaped = values.reshape(values.shape[0], heads, HEAD_DIM)
    freqs = 10000.0 ** (-(jnp.arange(HALF).astype(jnp.float32) * 2.0) / HEAD_DIM)
    angles = positions[:, None] * freqs[None, :]
    cosine = jnp.cos(angles)[:, None, :]
    sine = jnp.sin(angles)[:, None, :]
    first = shaped[:, :, :HALF]
    second = shaped[:, :, HALF:]
    return jnp.concatenate(
        [first * cosine - second * sine, second * cosine + first * sine], axis=2
    )


def general(dp, ctx, tokens, norm_gain, q_weight, k_weight, v_weight):
    rows = tokens.shape[1]
    heads = HEADS // ctx
    cols = heads * HEAD_DIM
    me = lax.axis_index("ctx")
    part = jnp.concatenate(
        [lax.dynamic_slice_in_dim(w, me * cols, cols, 1) for w in (q_weight, k_weight, v_weight)], axis=1
    )
    weights = lax.all_gather(part, "dp", axis=0, tiled=True)
    whole = lax.all_gather(tokens[0], "ctx", axis=0, tiled=True)
    normed = normalize(whole, norm_gain[None, :])
    linear = jnp.dot(normed, weights, preferred_element_type=jnp.float32)
    length = ctx * rows
    positions = jnp.arange(length).astype(jnp.float32)
    q = rotate(linear[:, :cols], positions).astype(jnp.bfloat16)
    k = rotate(linear[:, cols : 2 * cols], positions).astype(jnp.bfloat16)
    v = linear[:, 2 * cols :].astype(jnp.bfloat16).reshape(length, heads, HEAD_DIM)
    allowed = jnp.arange(length)[None, :] <= jnp.arange(length)[:, None]
    scores = jnp.einsum("qhd,khd->hqk", q, k, preferred_element_type=jnp.float32) * HEAD_DIM ** (-0.5)
    scores = jnp.where(allowed[None], scores, -1e30)
    top = jnp.max(scores, axis=2, keepdims=True)
    expo = jnp.where(allowed[None], jnp.exp(scores - top), 0.0)
    numer = jnp.einsum("hqk,khd->hqd", expo.astype(jnp.bfloat16), v, preferred_element_type=jnp.float32)
    result = (numer / jnp.sum(expo, axis=2, keepdims=True)).astype(jnp.bfloat16)
    result = result.reshape(heads, ctx, rows, HEAD_DIM).transpose(1, 2, 0, 3).reshape(ctx, rows, cols)
    back = lax.all_to_all(result, "ctx", 0, 0)
    return back.transpose(1, 0, 2).reshape(1, rows, ctx * cols)


def solution(mesh):
    dp, ctx = mesh.shape["dp"], mesh.shape["ctx"]
    body = fast if (dp, ctx) == (8, 4) else general
    placed = (P("dp", "ctx", None), P(), P("dp", None), P("dp", None), P("dp", None))
    return jax.shard_map(
        functools.partial(body, dp, ctx),
        mesh=mesh,
        in_specs=placed,
        out_specs=P("dp", "ctx", None),
        check_vma=False,
    )
```
